256 devices in a mesh: gx: 16 (over y, z_hi), gy: 16 (over z_lo, x, core).
Axes of the slice: x: 4, y: 4, z: 8 (z_hi: 4, z_lo: 2; z = z_hi * 2 + z_lo), core: 2. Of those that a mesh axis runs over, the one named last changes fastest.
Arguments:
- ensemble: float32 [80, 4, 128, 2048], P(None, None, 'gx', 'gy'), may hold values from -6 to 6
- obs_x: int32 [2, 1024], replicated, may hold values from 0 to 7
- obs_y: int32 [2, 1024], replicated, may hold values from 0 to 127
- obs_level: int32 [2, 1024], replicated, may hold values from 0 to 3
- owner_row: int32 [2], replicated, may hold values from 0 to 15
- owner_col: int32 [2], replicated, may hold values from 0 to 15
- obs_value: float32 [2, 1024], replicated, may hold values from -6 to 6
- obs_noise: float32 [2, 80, 1024], replicated, may hold values from -5 to 5
- obs_var: float32 [2, 1024], replicated, may hold values from 0.25 to 4
Outputs:
- posterior: float32 [80, 4, 128, 2048], P(None, None, 'gx', 'gy')
The draws below stay inside these ranges and needn't reach their ends.
Inputs may be any that keep to these rules, and one draw needn't show every extreme that they name: `owner_row`: gx index of the tile holding batch b's observations. `owner_col`: gy index of the tile holding batch b's observations.
All inputs are finite; a program needn't handle non-finite values.
Results may differ from the reference program's by a relative error of at most 0.0003.
Values sent between devices are 32-bit elements; how exact they have to be, the bound alone decides.
A program may use at most 128 MiB of HBM per device.

```python
import math
import jax
import jax.numpy as jnp
from jax import lax

K = 80
NOBS = 1024
NB = 2
NV = 4
LOC = 64
CX = 8
CY = 128
NX = 128
NY = 2048
N_GX = 16
N_GY = 16


def place_ends(result, stream_key, least, top_value):
    place = [jax.random.randint(jax.random.fold_in(stream_key, axis), (), 0, length) for axis, length in enumerate(result.shape)]
    widest = result.shape.index(max(result.shape))
    neighbour = place[:widest] + [(place[widest] + 1) % result.shape[widest]] + place[widest + 1:]
    return result.at[tuple(place)].set(least).at[tuple(neighbour)].set(top_value)


def block_scale(stream_key, dims, pieces, low, largest):
    def one(position, parts):
        draws = jax.random.uniform(jax.random.fold_in(jax.random.fold_in(stream_key, 6), position), (parts,), jnp.float32, low / len(pieces), largest / len(pieces))
        return jnp.repeat(jnp.exp(draws), dims[position] // parts).reshape((-1,) + (1,) * (len(dims) - position - 1))

    level = one(*pieces[0])
    for cut in pieces[1:]:
        level = level * one(*cut)
    return level


def scatter_about(stream_key, dims, spread, limit, shards=(), kind=jnp.bfloat16):
    array = jax.random.normal(stream_key, dims, jnp.float32) * spread
    if len(shards) > 0:
        array = block_scale(stream_key, dims, shards, -0.22, 0.18) * array
    return jnp.clip(array, min=-limit, max=limit).astype(kind)


def setup_inputs(seed: int = 0) -> dict:
    splits = jax.random.split(jax.random.key(seed), 10)
    ensemble = scatter_about(splits[0], (K, NV, NX, NY), 1.0, 6.0, ((2, 16), (3, 16)), jnp.float32)
    obs_x = place_ends(jax.random.randint(splits[1], (NB, NOBS), 0, CX), jax.random.fold_in(splits[1], 1), 0, CX - 1).astype(jnp.int32)
    obs_y = place_ends(jax.random.randint(splits[2], (NB, NOBS), 0, CY), jax.random.fold_in(splits[2], 1), 0, CY - 1).astype(jnp.int32)
    obs_level = place_ends(jax.random.randint(splits[3], (NB, NOBS), 0, NV), jax.random.fold_in(splits[3], 1), 0, NV - 1).astype(jnp.int32)
    owner_row = jax.random.randint(splits[4], (NB,), 0, N_GX).astype(jnp.int32)
    owner_col = jax.random.randint(splits[5], (NB,), 0, N_GY).astype(jnp.int32)
    obs_value = scatter_about(splits[6], (NB, NOBS), 1.0, 6.0, (), jnp.float32)
    obs_noise = scatter_about(splits[7], (NB, K, NOBS), 0.7, 5.0, (), jnp.float32)
    obs_var = jnp.clip(jnp.exp(jax.random.uniform(splits[8], (NB, NOBS), jnp.float32, math.log(0.25), math.log(4.0))), 0.25, 4.0)
    return {"ensemble": ensemble, "obs_x": obs_x, "obs_y": obs_y, "obs_level": obs_level, "owner_row": owner_row, "owner_col": owner_col, "obs_value": obs_value, "obs_noise": obs_noise, "obs_var": obs_var}


HIGH = lax.Precision.HIGHEST

def taper_of(dx, dy, dlev):
    dist = (dx * dx + dy * dy).astype(jnp.float32) / jnp.float32(LOC * LOC)
    inner = jnp.maximum(jnp.float32(1.0) - dist, jnp.float32(0.0))
    return inner * inner / (jnp.float32(1.0) + jnp.abs(dlev).astype(jnp.float32))

def solve_weights(obs_anom, innovation, variance, members):
    cov = jnp.dot(obs_anom.T.astype(jnp.float32), obs_anom.astype(jnp.float32), precision=HIGH, preferred_element_type=jnp.float32) / (members - 1)
    cov = cov + jnp.diag(variance)
    lower = jnp.linalg.cholesky(cov)
    half = jax.scipy.linalg.solve_triangular(lower, innovation.T, lower=True)
    whole = jax.scipy.linalg.solve_triangular(lower.T, half, lower=False)
    return whole.T

def reference(ensemble, obs_x, obs_y, obs_level, owner_row, owner_col, obs_value, obs_noise, obs_var):
    state = ensemble
    width_x = min(NX, CX + 2 * LOC)
    width_y = min(NY, CY + 2 * LOC)
    for batch in range(NB):
        glob_x = (owner_row[batch] * CX + obs_x[batch]).astype(jnp.int32)
        glob_y = (owner_col[batch] * CY + obs_y[batch]).astype(jnp.int32)
        levels = obs_level[batch]
        prior_hx = state[:, levels, glob_x, glob_y]
        obs_anom = prior_hx - jnp.mean(prior_hx, axis=0)
        innovation = obs_value[batch][None, :] + obs_noise[batch] - prior_hx
        weights = solve_weights(obs_anom, innovation, obs_var[batch], K)
        start_x = jnp.clip(owner_row[batch] * CX - LOC, 0, NX - width_x).astype(jnp.int32)
        start_y = jnp.clip(owner_col[batch] * CY - LOC, 0, NY - width_y).astype(jnp.int32)
        zero = jnp.int32(0)
        window = lax.dynamic_slice(state, (zero, zero, start_x, start_y), (K, NV, width_x, width_y))
        anomaly = window - jnp.mean(window, axis=0)
        lev_ids = jnp.arange(NV, dtype=jnp.int32)
        col_ids = start_y + jnp.arange(width_y, dtype=jnp.int32)

        def row_update(row):
            slab = lax.dynamic_index_in_dim(anomaly, row, axis=2, keepdims=False).reshape(K, NV * width_y)
            cross = jnp.dot(slab.T.astype(jnp.float32), obs_anom.astype(jnp.float32), precision=HIGH, preferred_element_type=jnp.float32) / (K - 1)
            dx = start_x + row - glob_x
            dy = col_ids[:, None] - glob_y[None, :]
            dlev = lev_ids[:, None, None] - levels[None, None, :]
            taper = taper_of(dx[None, None, :], dy[None, :, :], dlev).reshape(NV * width_y, NOBS)
            change = jnp.dot(weights.astype(jnp.float32), (taper * cross).T.astype(jnp.float32), precision=HIGH, preferred_element_type=jnp.float32)
            return change.reshape(K, NV, width_y)
        change = lax.map(row_update, jnp.arange(width_x, dtype=jnp.int32))
        change = jnp.transpose(change, (1, 2, 0, 3))
        state = lax.dynamic_update_slice(state, window + change, (zero, zero, start_x, start_y))
    return state
```

```python
import jax
import jax.numpy as jnp
from jax import lax
from jax.experimental import pallas as pl
from jax.experimental.pallas import tpu as pltpu
from jax.sharding import PartitionSpec as P

HIGH = lax.Precision.HIGHEST
F32 = jnp.float32
BF16 = jnp.bfloat16
LOC = 64
MEMBERS = 80
NT = (((1,), (1,)), ((), ()))
NN = (((1,), (0,)), ((), ()))


def split(v):
    hi = v.astype(BF16)
    lo = (v - hi.astype(F32)).astype(BF16)
    return hi, lo


def dot(a, b, dims=NN, precision=None):
    return lax.dot_general(a, b, dims, precision=precision, preferred_element_type=F32)


def pick_kernel(place, state, ox, oy, ol, out):
    gx = lax.axis_index("gx")
    gy = lax.axis_index("gy")
    for b in range(2):
        owned = jnp.logical_and(place[0, b] == gx, place[1, b] == gy)

        @pl.when(owned)
        def _():
            @pl.loop(0, 8)
            def _(c):
                cols = pl.ds(pl.multiple_of(c * 128, 128), 128)
                want = ol[b : b + 1, cols] * 8 + ox[b : b + 1, cols]
                at = jnp.broadcast_to(oy[b : b + 1, cols], (MEMBERS, 128))
                got = jnp.zeros((MEMBERS, 128), F32)
                for row in range(32):
                    cells = state[pl.ds(row, MEMBERS, stride=32), :]
                    moved = jnp.take_along_axis(cells, at, axis=1)
                    got = jnp.where(want == row, moved, got)
                out[b, c] = got

        @pl.when(jnp.logical_not(owned))
        def _():
            out[b] = jnp.zeros((8, MEMBERS, 128), F32)


def invert(m):
    rows = lax.broadcasted_iota(jnp.int32, (MEMBERS, 1), 0)
    lanes = lax.broadcasted_iota(jnp.int32, (1, 128), 1)
    for j in range(0, MEMBERS, 2):
        r0, r1 = m[j : j + 1], m[j + 1 : j + 2]
        a, b, d = r0[:, j : j + 1], r0[:, j + 1 : j + 2], r1[:, j + 1 : j + 2]
        scale = 1.0 / (a * d - b * b)
        i00, i01, i11 = d * scale, -b * scale, a * scale
        c0, c1 = m[:, j : j + 1], m[:, j + 1 : j + 2]
        first, second = lanes == j, lanes == j + 1
        both = jnp.logical_or(first, second)
        r0 = jnp.where(both, jnp.where(first, 1.0, 0.0), r0)
        r1 = jnp.where(both, jnp.where(second, 1.0, 0.0), r1)
        s0 = i00 * r0 + i01 * r1
        s1 = i01 * r0 + i11 * r1
        top, low = rows == j, rows == j + 1
        c0 = jnp.where(top, -1.0, jnp.where(low, 0.0, c0))
        c1 = jnp.where(low, -1.0, jnp.where(top, 0.0, c1))
        rest = jnp.where(jnp.logical_or(both, jnp.logical_or(top, low)), 0.0, m)
        m = rest - c0 * s0 - c1 * s1
    return m


def update_kernel(place, state, obs, ox, oy, ol, value, noise, var, out,
                  held, both, scaled, cast, weights, near_y, col_x, col_y, col_l, taper, hx, sem):
    gx = lax.axis_index("gx")
    gy = lax.axis_index("gy")
    load = pltpu.make_async_copy(state, out, sem)
    load.start()

    def close(b, x, y):
        return jnp.logical_and(jnp.abs(x - place[0, b]) <= 8, jnp.abs(y - place[1, b]) <= 1)

    near = [close(b, gx, gy) for b in range(2)]
    linked = jnp.logical_and(near[1], close(0, place[0, 1], place[1, 1]))
    hx[...] = obs[...]

    def prepare(b):
        for c in range(8):
            cols = slice(c * 128, c * 128 + 128)
            h = hx[b, c]
            o = h - jnp.sum(h, axis=0, keepdims=True) * (1.0 / MEMBERS)
            d = value[b : b + 1, cols] + noise[b, :, cols] - h
            both[0:MEMBERS, cols] = o
            both[MEMBERS : 2 * MEMBERS, cols] = d
            scaled[:, cols] = o * (1.0 / var[b : b + 1, cols])
            three = jnp.concatenate([o, o, o, jnp.zeros((16, 128), F32)], axis=0)
            held[cols, 0:128] = three[0:128].T
            held[cols, 128:256] = three[128:256].T
            for ref, dst in ((ox, col_x), (oy, col_y), (ol, col_l)):
                dst[cols, :] = jnp.broadcast_to(ref[b : b + 1, cols].astype(F32), (128, 128)).T
        gram = dot(both[...], scaled[...], NT, HIGH)
        inner = jnp.concatenate([gram[0:MEMBERS], jnp.zeros((MEMBERS, 48), F32)], axis=1)
        eye = lax.broadcasted_iota(jnp.int32, (MEMBERS, 128), 0) == lax.broadcasted_iota(
            jnp.int32, (MEMBERS, 128), 1
        )
        inner = inner + jnp.where(eye, MEMBERS - 1.0, 0.0)
        inverse = invert(inner)
        factor = dot(gram[MEMBERS : 2 * MEMBERS], inverse[:, 0:MEMBERS], NN, HIGH)
        w = both[MEMBERS : 2 * MEMBERS] - dot(factor, both[0:MEMBERS], NN, HIGH)
        w = w * (1.0 / var[b : b + 1, :])
        hi, lo = split(w)
        weights[0:MEMBERS] = hi
        weights[MEMBERS : 2 * MEMBERS] = lo
        lane = lax.broadcasted_iota(jnp.int32, (1, 128), 1)
        mesh_y = (gy * 128 + lane).astype(F32) - (place[1, b] * 128).astype(F32)

        @pl.loop(0, 8)
        def _(c):
            cols = pl.ds(pl.multiple_of(c * 128, 128), 128)
            dy = mesh_y - col_y[cols, :]
            near_y[cols, :] = 1.0 - dy * dy * (1.0 / (LOC * LOC))
            for level in range(4):
                gap = jnp.abs(level - col_l[cols, :])
                factor_l = (1.0 / (1.0 + gap)) * (1.0 / (MEMBERS - 1))
                for half in range(2):
                    part = held[cols, half * 128 : half * 128 + 128] * factor_l
                    hi, lo = split(part)
                    if half == 1:
                        hi = jnp.where(lane < 32, hi.astype(F32), lo.astype(F32)).astype(BF16)
                    cast[level, cols, half * 128 : half * 128 + 128] = hi

    def gain(values, level, taper_at):
        mean = jnp.sum(values, axis=0, keepdims=True) * (1.0 / MEMBERS)
        hi, lo = split(values - mean)
        right = jnp.concatenate([hi, lo, hi, jnp.zeros((16, values.shape[1]), BF16)], axis=0)
        total = jnp.zeros((2 * MEMBERS, values.shape[1]), F32)
        rest = jnp.zeros((MEMBERS, values.shape[1]), F32)
        for part in range(4):
            span = slice(part * 256, part * 256 + 256)
            cross = dot(cast[level, span, :], right)
            hi, lo = split(cross * taper_at(span))
            total = total + dot(weights[:, span], hi)
            rest = rest + dot(weights[0:MEMBERS, span], lo)
        return total[0:MEMBERS] + total[MEMBERS : 2 * MEMBERS] + rest

    def move_state(b):
        @pl.loop(0, 4)
        def _(pair):
            for half in range(2):
                x = (gx * 8 + pair * 2 + half).astype(F32) - (place[0, b] * 8).astype(F32)

                @pl.loop(0, 8)
                def _(c):
                    cols = pl.ds(pl.multiple_of(c * 128, 128), 128)
                    dx = x - col_x[cols, :]
                    t = jnp.maximum(near_y[cols, :] - dx * dx * (1.0 / (LOC * LOC)), 0.0)
                    taper[cols, half * 128 : half * 128 + 128] = t * t

            @pl.loop(0, 4)
            def _(level):
                rows = [pl.ds(level * 8 + pair * 2 + half, MEMBERS, stride=32) for half in range(2)]
                cells = [out[r, :] for r in rows]
                change = gain(jnp.concatenate(cells, axis=1), level, lambda span: taper[span, :])
                for half in range(2):
                    out[rows[half], :] = cells[half] + change[:, half * 128 : half * 128 + 128]

    def move_obs():
        @pl.loop(0, 8)
        def _(c):
            cols = pl.ds(pl.multiple_of(c * 128, 128), 128)
            x = (ox[1:2, cols] + (place[0, 1] - place[0, 0]) * 8).astype(F32)
            y = (oy[1:2, cols] + (place[1, 1] - place[1, 0]) * 128).astype(F32)
            lev = ol[1:2, cols].astype(F32)

            def taper_at(span):
                dx = x - col_x[span, :]
                dy = y - col_y[span, :]
                t = jnp.maximum(1.0 - (dx * dx + dy * dy) * (1.0 / (LOC * LOC)), 0.0)
                gap = jnp.abs(col_l[span, :] - lev)
                own = jnp.abs(col_l[span, :])
                return t * t * (1.0 + own) / (1.0 + gap)

            h = hx[1, c]
            hx[1, c] = h + gain(h, 0, taper_at)

    @pl.when(jnp.logical_or(near[0], linked))
    def _():
        prepare(0)

    load.wait()

    @pl.when(near[0])
    def _():
        move_state(0)

    @pl.when(linked)
    def _():
        move_obs()

    @pl.when(near[1])
    def _():
        prepare(1)
        move_state(1)


VMEM = pl.BlockSpec(memory_space=pltpu.VMEM)
SMEM = pl.BlockSpec(memory_space=pltpu.SMEM)
ANY = pl.BlockSpec(memory_space=pl.ANY)


def pick(place, state, ox, oy, ol):
    return pl.pallas_call(
        pick_kernel,
        out_shape=jax.ShapeDtypeStruct((2, 8, MEMBERS, 128), F32),
        in_specs=[SMEM, VMEM, VMEM, VMEM, VMEM],
        out_specs=VMEM,
        compiler_params=pltpu.CompilerParams(vmem_limit_bytes=48 * 2**20),
    )(place, state, ox, oy, ol)


def update(place, state, obs, ox, oy, ol, value, noise, var):
    S = pltpu.VMEM
    return pl.pallas_call(
        update_kernel,
        out_shape=jax.ShapeDtypeStruct(state.shape, F32),
        in_specs=[SMEM, ANY] + [VMEM] * 7,
        out_specs=VMEM,
        scratch_shapes=[
            S((1024, 256), F32),
            S((160, 1024), F32),
            S((MEMBERS, 1024), F32),
            S((4, 1024, 256), BF16),
            S((160, 1024), BF16),
            S((1024, 128), F32),
            S((1024, 128), F32),
            S((1024, 128), F32),
            S((1024, 128), F32),
            S((1024, 256), F32),
            S((2, 8, MEMBERS, 128), F32),
            pltpu.SemaphoreType.DMA,
        ],
        compiler_params=pltpu.CompilerParams(vmem_limit_bytes=56 * 2**20),
    )(place, state, obs, ox, oy, ol, value, noise, var)


MESH = pl.DeviceIdType.MESH

def spread_kernel(piece, out, pair_buf, acc, ring_buf, z_src, z_buf,
                  s0s, s0r, s1s, s1r, s2s, s2r, s3s, s3r, s4s, s4r):
    gx = lax.axis_index("gx")
    gy = lax.axis_index("gy")
    yy = gx // 4
    zh = gx % 4
    zl = gy // 8
    xx = (gy // 2) % 4
    core = gy % 2
    other = 1 - core
    q = yy * 4 + xx
    z = zh * 2 + zl

    def dev_xy(t):
        return ((t // 4) * 4 + zh, zl * 8 + (t % 4) * 2 + core)

    def dev_z(t):
        return (yy * 4 + t // 2, (t % 2) * 8 + xx * 2 + core)

    mate = (gx, zl * 8 + xx * 2 + other)

    barrier = pltpu.get_barrier_semaphore()

    @pl.loop(1, 16)
    def _(d):
        pl.semaphore_signal(barrier, inc=1, device_id=dev_xy((q + d) % 16), device_id_type=MESH)

    @pl.loop(1, 8)
    def _(d):
        pl.semaphore_signal(barrier, inc=1, device_id=dev_z((z + d) % 8), device_id_type=MESH)

    pl.semaphore_signal(barrier, inc=1, device_id=mate, device_id_type=MESH)
    pl.semaphore_wait(barrier, 23)

    def c0(t):
        return pltpu.make_async_remote_copy(
            src_ref=piece.at[other, t], dst_ref=pair_buf.at[t], send_sem=s0s.at[t], recv_sem=s0r.at[t],
            device_id=mate, device_id_type=MESH)

    def c1(t, slot):
        return pltpu.make_async_remote_copy(
            src_ref=acc.at[t], dst_ref=ring_buf.at[slot], send_sem=s1s.at[t], recv_sem=s1r.at[slot],
            device_id=dev_xy(t), device_id_type=MESH)

    def c2(t, slot):
        return pltpu.make_async_remote_copy(
            src_ref=z_src, dst_ref=z_buf.at[slot], send_sem=s2s.at[t], recv_sem=s2r.at[slot],
            device_id=dev_z(t), device_id_type=MESH)

    def c3(t, slot):
        return pltpu.make_async_remote_copy(
            src_ref=out.at[core, slot], dst_ref=out.at[core, slot], send_sem=s3s.at[t], recv_sem=s3r.at[slot],
            device_id=dev_xy(t), device_id_type=MESH)

    def c4(w, slot):
        return pltpu.make_async_remote_copy(
            src_ref=out.at[w, slot], dst_ref=out.at[w, slot], send_sem=s4s.at[slot], recv_sem=s4r.at[slot],
            device_id=mate, device_id_type=MESH)

    @pl.loop(1, 17)
    def _(d):
        c0((q + d) % 16).start()

    @pl.loop(1, 16)
    def _(d):
        t = (q + d) % 16
        c0(t).wait_recv()
        acc[t] = piece[core, t] + pair_buf[t]
        c1(t, q).start()

    c0(q).wait_recv()
    z_src[...] = piece[core, q] + pair_buf[q]

    @pl.loop(1, 16)
    def _(d):
        t = (q + 16 - d) % 16
        c1(t, t).wait_recv()
        z_src[...] += ring_buf[t]

    @pl.loop(1, 8)
    def _(d):
        c2((z + d) % 8, z).start()

    out[core, q] = z_src[...]

    @pl.loop(1, 8)
    def _(d):
        t = (z + 8 - d) % 8
        c2(t, t).wait_recv()
        out[core, q] += z_buf[t]

    @pl.loop(1, 16)
    def _(d):
        c3((q + d) % 16, q).start()

    c4(core, q).start()

    @pl.loop(1, 16)
    def _(d):
        t = (q + 16 - d) % 16
        c3(t, t).wait_recv()
        c4(core, t).start()

    @pl.loop(0, 16)
    def _(d):
        c4(other, (q + 16 - d) % 16).wait_recv()

    @pl.loop(0, 16)
    def _(t):
        c0(t).wait_send()
        c4(core, t).wait_send()

    @pl.loop(1, 16)
    def _(d):
        t = (q + d) % 16
        c1(t, q).wait_send()
        c3(t, q).wait_send()

    @pl.loop(1, 8)
    def _(d):
        c2((z + d) % 8, z).wait_send()


def spread(piece):
    D = pltpu.SemaphoreType.DMA
    return pl.pallas_call(
        spread_kernel,
        out_shape=jax.ShapeDtypeStruct((2, 16, 40, 128), jnp.float32),
        in_specs=[pl.BlockSpec(memory_space=pltpu.VMEM)],
        out_specs=pl.BlockSpec(memory_space=pltpu.VMEM),
        scratch_shapes=[
            pltpu.VMEM((16, 40, 128), jnp.float32),
            pltpu.VMEM((16, 40, 128), jnp.float32),
            pltpu.VMEM((16, 40, 128), jnp.float32),
            pltpu.VMEM((40, 128), jnp.float32),
            pltpu.VMEM((8, 40, 128), jnp.float32),
            D((16,)), D((16,)), D((16,)), D((16,)), D((8,)), D((8,)), D((16,)), D((16,)), D((16,)), D((16,)),
        ],
        compiler_params=pltpu.CompilerParams(collective_id=0, has_side_effects=True),
    )(piece)


def shards(ensemble, obs_x, obs_y, obs_level, owner_row, owner_col, obs_value, obs_noise, obs_var):
    place = jnp.stack([owner_row, owner_col])
    state = ensemble.reshape(-1, ensemble.shape[3])
    piece = pick(place, state, obs_x, obs_y, obs_level)
    obs = spread(piece.reshape(2, 16, 40, 128)).reshape(2, 8, MEMBERS, 128)
    out = update(place, state, obs, obs_x, obs_y, obs_level, obs_value, obs_noise, obs_var)
    return out.reshape(ensemble.shape)


def solution(mesh):
    in_specs = (P(None, None, "gx", "gy"), P(), P(), P(), P(), P(), P(), P(), P())
    out_specs = P(None, None, "gx", "gy")
    return jax.shard_map(shards, mesh=mesh, in_specs=in_specs, out_specs=out_specs, check_vma=False)
```

```python
import jax
import jax.numpy as jnp
from jax import lax
from jax.experimental import pallas as pl
from jax.experimental.pallas import tpu as pltpu
from jax.sharding import PartitionSpec as P

HIGH = lax.Precision.HIGHEST
F32 = jnp.float32
BF16 = jnp.bfloat16
LOC = 64
MEMBERS = 80
NT = (((1,), (1,)), ((), ()))
NN = (((1,), (0,)), ((), ()))


def split(v):
    hi = v.astype(BF16)
    lo = (v - hi.astype(F32)).astype(BF16)
    return hi, lo


def dot(a, b, dims=NN, precision=None):
    return lax.dot_general(a, b, dims, precision=precision, preferred_element_type=F32)


def pick_kernel(row_in, col_in, state, ox_in, oy_in, ol_in, out, row, col, ox, oy, ol, cells, sem, sem_cells):
    gx = lax.axis_index("gx")
    gy = lax.axis_index("gy")
    small = [(row_in, row), (col_in, col), (ox_in, ox), (oy_in, oy), (ol_in, ol)]
    small = [pltpu.make_async_copy(src, dst, sem.at[i]) for i, (src, dst) in enumerate(small)]
    for copy in small:
        copy.start()
    small[0].wait()
    small[1].wait()
    owned = [jnp.logical_and(row[b] == gx, col[b] == gy) for b in range(2)]

    @pl.when(jnp.logical_or(owned[0], owned[1]))
    def _():
        @pl.loop(0, 32)
        def _(r):
            pltpu.make_async_copy(state.at[:, r], cells.at[r], sem_cells).start()

    for copy in small[2:]:
        copy.wait()

    @pl.when(jnp.logical_or(owned[0], owned[1]))
    def _():
        pltpu.make_async_copy(cells, cells, sem_cells).wait()

    for b in range(2):

        @pl.when(owned[b])
        def _():
            @pl.loop(0, 8)
            def _(c):
                cols = pl.ds(pl.multiple_of(c * 128, 128), 128)
                want = jnp.broadcast_to(ol[b : b + 1, cols] * 8 + ox[b : b + 1, cols], (8, 128))
                at = jnp.broadcast_to(oy[b : b + 1, cols], (8, 128))
                for k in range(0, MEMBERS, 8):
                    got = jnp.zeros((8, 128), F32)
                    for r in range(32):
                        moved = jnp.take_along_axis(cells[r, k : k + 8], at, axis=1, mode="promise_in_bounds")
                        got = jnp.where(want == r, moved, got)
                    out[b, c, k : k + 8] = got

        @pl.when(jnp.logical_not(owned[b]))
        def _():
            out[b] = jnp.zeros((8, MEMBERS, 128), F32)


def inverse_of(a, keep):
    eye = jnp.where(
        lax.broadcasted_iota(jnp.int32, a.shape, 0) == lax.broadcasted_iota(jnp.int32, a.shape, 1), 1.0, 0.0
    )
    top = jnp.max(jnp.sum(jnp.abs(a), axis=1, keepdims=True), axis=0, keepdims=True)
    scale = 2.0 / (top + (MEMBERS - 1.0))
    r = eye - scale * a
    x = scale * (eye + r)
    for _ in range(5):
        r = dot(r, r, NN, HIGH)
        x = x + dot(x, r, NN, HIGH)

    keep[0] = x
    keep[1] = r

    def more(held):
        return jnp.logical_and(held[0] > 1e-4, held[1] < 40)

    def rest(held):
        r = dot(keep[1], keep[1], NN, HIGH)
        keep[0] = keep[0] + dot(keep[0], r, NN, HIGH)
        keep[1] = r
        return jnp.max(jnp.abs(r)), held[1] + 1

    _, count = lax.while_loop(more, rest, (jnp.max(jnp.abs(r)), jnp.int32(0)))

    @pl.when(count > 0)
    def _():
        x = keep[0]
        keep[0] = x + dot(x, eye - dot(a, x, NN, HIGH), NN, HIGH)

    return keep[0]


def update_kernel(row_in, col_in, state, obs, ox_in, oy_in, ol_in, value_in, noise_in, var_in, out,
                  row, col, ox, oy, ol, value, var, cells, hx, noises, both, scaled, cast, weights, near_y, col_x, col_y, col_f, taper, keep, gain_hi, gain_lo,
                  sem_in, sem_obs, sem_out):
    gx = lax.axis_index("gx")
    gy = lax.axis_index("gy")
    small = [(row_in, row), (col_in, col), (ox_in, ox), (oy_in, oy), (ol_in, ol), (value_in, value), (var_in, var)]
    small += [(obs, hx), (noise_in, noises)]
    small = [pltpu.make_async_copy(src, dst, sem_obs.at[i]) for i, (src, dst) in enumerate(small)]
    for copy in small[:2]:
        copy.start()
    for copy in small[:2]:
        copy.wait()

    def close(b, x, y):
        return jnp.logical_and(jnp.abs(x - row[b]) <= 8, jnp.abs(y - col[b]) <= 1)

    near = [close(b, gx, gy) for b in range(2)]
    linked = jnp.logical_and(near[1], close(0, row[1], col[1]))
    any_near = jnp.logical_or(near[0], near[1])
    whole = pltpu.make_async_copy(state, out, sem_out)
    all_in = pltpu.make_async_copy(cells, cells, sem_in)
    all_out = pltpu.make_async_copy(cells, cells, sem_out)

    def fetch(r):
        return pltpu.make_async_copy(state.at[:, r], cells.at[r], sem_in)

    def store(r):
        return pltpu.make_async_copy(cells.at[r], out.at[:, r], sem_out)

    @pl.when(any_near)
    def _():
        for copy in small[2:]:
            copy.start()

        @pl.loop(0, 32)
        def _(r):
            fetch(r).start()

        for copy in small[2:]:
            copy.wait()

    @pl.when(jnp.logical_not(any_near))
    def _():
        whole.start()
        whole.wait()

    def prepare(b):
        lane = lax.broadcasted_iota(jnp.int32, (1, 128), 1)
        mesh_y = (gy * 128 + lane - col[b] * 128).astype(F32) * (1.0 / LOC)

        @pl.loop(0, 8)
        def _(c):
            cols = pl.ds(pl.multiple_of(c * 128, 128), 128)
            h = hx[b, c]
            inv = 1.0 / var[b : b + 1, cols]
            o = h - jnp.sum(h, axis=0, keepdims=True) * (1.0 / MEMBERS)
            d = value[b : b + 1, cols] + noises[b, :, cols] - h
            both[0:MEMBERS, cols] = o
            both[MEMBERS : 2 * MEMBERS, cols] = d
            scaled[:, cols] = o * inv
            lev = ol[b : b + 1, cols].astype(F32)
            extra = [ox[b : b + 1, cols].astype(F32) * (1.0 / LOC), oy[b : b + 1, cols].astype(F32) * (1.0 / LOC)]
            for level in range(4):
                extra.append(1.0 / ((1.0 + jnp.abs(level - lev)) * (MEMBERS - 1)))
            extra.append(jnp.zeros((42, 128), F32))
            turned = jnp.concatenate([o] + extra, axis=0).T
            x_at = jnp.broadcast_to(turned[:, 80:81], (128, 128))
            y_at = jnp.broadcast_to(turned[:, 81:82], (128, 128))
            col_x[cols, :] = x_at
            col_y[cols, :] = y_at
            dy = mesh_y - y_at
            near_y[cols, :] = 1.0 - dy * dy
            turned_o = jnp.where(lane < MEMBERS, turned, 0.0)
            first = turned_o + jnp.where(lane >= MEMBERS, pltpu.roll(turned, MEMBERS, 1), 0.0)
            second = jnp.where(lane < 32, pltpu.roll(turned, MEMBERS, 1), 0.0) + pltpu.roll(turned_o, 32, 1)
            for level in range(5):
                if level < 4:
                    f_at = jnp.broadcast_to(turned[:, 82 + level : 83 + level], (128, 128))
                    col_f[level, cols, :] = f_at
                    left, right = first * f_at, second * f_at
                else:
                    left, right = first, second
                hi = right.astype(BF16).astype(F32)
                cast[level, cols, 0:128] = left.astype(BF16)
                cast[level, cols, 128:256] = jnp.where(lane < 32, hi, right - hi).astype(BF16)

        gram = dot(both[...], scaled[...], NT, HIGH)
        inner = gram[0:MEMBERS]
        eye = lax.broadcasted_iota(jnp.int32, (MEMBERS, MEMBERS), 0) == lax.broadcasted_iota(
            jnp.int32, (MEMBERS, MEMBERS), 1
        )
        trace = jnp.sum(jnp.sum(jnp.where(eye, inner, 0.0), axis=1, keepdims=True), axis=0, keepdims=True)
        inner = inner + jnp.where(eye, MEMBERS - 1.0, 0.0) + trace * (1.0 / MEMBERS / MEMBERS)
        inverse = inverse_of(inner, keep)
        factor = dot(gram[MEMBERS : 2 * MEMBERS], inverse, NN, HIGH)
        w = both[MEMBERS : 2 * MEMBERS] - dot(factor, both[0:MEMBERS], NN, HIGH)
        w = w * (1.0 / var[b : b + 1, :])
        hi, lo = split(w)
        weights[0:MEMBERS] = hi
        weights[MEMBERS : 2 * MEMBERS] = lo

    def spread_of(values):
        mean = jnp.sum(values, axis=0, keepdims=True) * (1.0 / MEMBERS)
        hi, lo = split(values - mean)
        return jnp.concatenate([hi, lo, hi, jnp.zeros((16, values.shape[1]), BF16)], axis=0)

    def gain(values, level, taper_at, slot=0):
        right = spread_of(values)
        wide = values.shape[1]
        for part in range(4):
            span = slice(part * 256, part * 256 + 256)
            cross = dot(cast[level, span, :], right)
            hi, lo = split(cross * taper_at(span))
            gain_hi[slot, span, 0:wide] = hi
            gain_lo[slot, span, 0:wide] = lo
        total = dot(weights[...], gain_hi[slot, :, 0:wide])
        rest = dot(weights[0:MEMBERS], gain_lo[slot, :, 0:wide])
        return total[0:MEMBERS] + total[MEMBERS : 2 * MEMBERS] + rest

    def move_state(b, last):
        @pl.loop(0, 4)
        def _(pair):
            for half in range(2):
                x = (gx * 8 + pair * 2 + half - row[b] * 8).astype(F32) * (1.0 / LOC)

                @pl.loop(0, 8)
                def _(c):
                    cols = pl.ds(pl.multiple_of(c * 128, 128), 128)
                    dx = x - col_x[cols, :]
                    t = jnp.maximum(near_y[cols, :] - dx * dx, 0.0)
                    taper[cols, half * 128 : half * 128 + 128] = t * t

            before = []
            for level in range(4):
                before.append([cells[level * 8 + pair * 2 + half] for half in range(2)])
            after = []
            for level in range(4):
                change = gain(jnp.concatenate(before[level], axis=1), level, lambda span: taper[span, :], level % 2)
                after.append([before[level][half] + change[:, half * 128 : half * 128 + 128] for half in range(2)])
            for level in range(4):
                for half in range(2):
                    cells[level * 8 + pair * 2 + half] = after[level][half]
            for level in range(4):
                for half in range(2):
                    r = level * 8 + pair * 2 + half
                    if last is True:
                        store(r).start()
                    else:
                        pl.when(last)(store(r).start)

    def move_obs():
        @pl.loop(0, 8)
        def _(c):
            cols = pl.ds(pl.multiple_of(c * 128, 128), 128)
            x = (ox[1:2, cols] + (row[1] - row[0]) * 8).astype(F32) * (1.0 / LOC)
            y = (oy[1:2, cols] + (col[1] - col[0]) * 128).astype(F32) * (1.0 / LOC)
            lev = ol[1:2, cols]

            def taper_at(span):
                dx = x - col_x[span, :]
                dy = y - col_y[span, :]
                t = jnp.maximum(1.0 - (dx * dx + dy * dy), 0.0)
                f = col_f[3, span, :]
                for level in range(3):
                    f = jnp.where(lev == level, col_f[level, span, :], f)
                return t * t * f

            h = hx[1, c]
            hx[1, c] = h + gain(h, 4, taper_at)

    @pl.when(jnp.logical_or(near[0], linked))
    def _():
        prepare(0)

    @pl.when(any_near)
    def _():
        all_in.wait()

    @pl.when(near[0])
    def _():
        move_state(0, jnp.logical_not(near[1]))

    @pl.when(linked)
    def _():
        move_obs()

    @pl.when(near[1])
    def _():
        prepare(1)
        move_state(1, True)

    @pl.when(any_near)
    def _():
        all_out.wait()


VMEM = pl.BlockSpec(memory_space=pltpu.VMEM)
SMEM = pl.BlockSpec(memory_space=pltpu.SMEM)
ANY = pl.BlockSpec(memory_space=pl.ANY)


def pick(row, col, state, ox, oy, ol):
    return pl.pallas_call(
        pick_kernel,
        out_shape=jax.ShapeDtypeStruct((2, 8, MEMBERS, 128), F32),
        in_specs=[ANY] * 6,
        out_specs=VMEM,
        scratch_shapes=[
            pltpu.SMEM((2,), jnp.int32),
            pltpu.SMEM((2,), jnp.int32),
            pltpu.VMEM((2, 1024), jnp.int32),
            pltpu.VMEM((2, 1024), jnp.int32),
            pltpu.VMEM((2, 1024), jnp.int32),
            pltpu.VMEM((32, MEMBERS, 128), F32),
            pltpu.SemaphoreType.DMA((5,)),
            pltpu.SemaphoreType.DMA,
        ],
        compiler_params=pltpu.CompilerParams(vmem_limit_bytes=60 * 2**20),
    )(row, col, state, ox, oy, ol)


def update(row, col, state, obs, ox, oy, ol, value, noise, var):
    S = pltpu.VMEM
    return pl.pallas_call(
        update_kernel,
        out_shape=jax.ShapeDtypeStruct(state.shape, F32),
        in_specs=[ANY] * 10,
        out_specs=ANY,
        scratch_shapes=[
            pltpu.SMEM((2,), jnp.int32),
            pltpu.SMEM((2,), jnp.int32),
            S((2, 1024), jnp.int32),
            S((2, 1024), jnp.int32),
            S((2, 1024), jnp.int32),
            S((2, 1024), F32),
            S((2, 1024), F32),
            S((32, MEMBERS, 128), F32),
            S((2, 8, MEMBERS, 128), F32),
            S((2, MEMBERS, 1024), F32),
            S((160, 1024), F32),
            S((MEMBERS, 1024), F32),
            S((5, 1024, 256), BF16),
            S((160, 1024), BF16),
            S((1024, 128), F32),
            S((1024, 128), F32),
            S((1024, 128), F32),
            S((4, 1024, 128), F32),
            S((1024, 256), F32),
            S((2, MEMBERS, MEMBERS), F32),
            S((2, 1024, 256), BF16),
            S((2, 1024, 256), BF16),
            pltpu.SemaphoreType.DMA,
            pltpu.SemaphoreType.DMA((9,)),
            pltpu.SemaphoreType.DMA,
        ],
        compiler_params=pltpu.CompilerParams(vmem_limit_bytes=60 * 2**20),
    )(row, col, state, obs, ox, oy, ol, value, noise, var)


MESH = pl.DeviceIdType.MESH

def spread_kernel(piece, out, pair_buf, acc, ring_buf, z_src, z_buf,
                  s0s, s0r, s1s, s1r, s2s, s2r, s3s, s3r, s4s, s4r):
    gx = lax.axis_index("gx")
    gy = lax.axis_index("gy")
    yy = gx // 4
    zh = gx % 4
    zl = gy // 8
    xx = (gy // 2) % 4
    core = gy % 2
    other = 1 - core
    q = yy * 4 + xx
    z = zh * 2 + zl

    def dev_xy(t):
        return ((t // 4) * 4 + zh, zl * 8 + (t % 4) * 2 + core)

    def dev_z(t):
        return (yy * 4 + t // 2, (t % 2) * 8 + xx * 2 + core)

    mate = (gx, zl * 8 + xx * 2 + other)

    barrier = pltpu.get_barrier_semaphore()

    @pl.loop(1, 16)
    def _(d):
        pl.semaphore_signal(barrier, inc=1, device_id=dev_xy((q + d) % 16), device_id_type=MESH)

    @pl.loop(1, 8)
    def _(d):
        pl.semaphore_signal(barrier, inc=1, device_id=dev_z((z + d) % 8), device_id_type=MESH)

    pl.semaphore_signal(barrier, inc=1, device_id=mate, device_id_type=MESH)
    pl.semaphore_wait(barrier, 23)

    def c0(t):
        return pltpu.make_async_remote_copy(
            src_ref=piece.at[other, t], dst_ref=pair_buf.at[t], send_sem=s0s.at[t], recv_sem=s0r.at[t],
            device_id=mate, device_id_type=MESH)

    def c1(t, slot):
        return pltpu.make_async_remote_copy(
            src_ref=acc.at[t], dst_ref=ring_buf.at[slot], send_sem=s1s.at[t], recv_sem=s1r.at[slot],
            device_id=dev_xy(t), device_id_type=MESH)

    def c2(t, slot):
        return pltpu.make_async_remote_copy(
            src_ref=z_src, dst_ref=z_buf.at[slot], send_sem=s2s.at[t], recv_sem=s2r.at[slot],
            device_id=dev_z(t), device_id_type=MESH)

    def c3(t, slot):
        return pltpu.make_async_remote_copy(
            src_ref=out.at[core, slot], dst_ref=out.at[core, slot], send_sem=s3s.at[t], recv_sem=s3r.at[slot],
            device_id=dev_xy(t), device_id_type=MESH)

    def c4(w, slot):
        return pltpu.make_async_remote_copy(
            src_ref=out.at[w, slot], dst_ref=out.at[w, slot], send_sem=s4s.at[slot], recv_sem=s4r.at[slot],
            device_id=mate, device_id_type=MESH)

    @pl.loop(1, 17)
    def _(d):
        c0((q + d) % 16).start()

    @pl.loop(1, 16)
    def _(d):
        t = (q + d) % 16
        c0(t).wait_recv()
        acc[t] = piece[core, t] + pair_buf[t]
        c1(t, q).start()

    c0(q).wait_recv()
    z_src[...] = piece[core, q] + pair_buf[q]

    @pl.loop(1, 16)
    def _(d):
        t = (q + 16 - d) % 16
        c1(t, t).wait_recv()
        z_src[...] += ring_buf[t]

    @pl.loop(1, 8)
    def _(d):
        c2((z + d) % 8, z).start()

    out[core, q] = z_src[...]

    @pl.loop(1, 8)
    def _(d):
        t = (z + 8 - d) % 8
        c2(t, t).wait_recv()
        out[core, q] += z_buf[t]

    @pl.loop(1, 16)
    def _(d):
        c3((q + d) % 16, q).start()

    c4(core, q).start()

    @pl.loop(1, 16)
    def _(d):
        t = (q + 16 - d) % 16
        c3(t, t).wait_recv()
        c4(core, t).start()

    @pl.loop(0, 16)
    def _(d):
        c4(other, (q + 16 - d) % 16).wait_recv()

    @pl.loop(0, 16)
    def _(t):
        c0(t).wait_send()
        c4(core, t).wait_send()

    @pl.loop(1, 16)
    def _(d):
        t = (q + d) % 16
        c1(t, q).wait_send()
        c3(t, q).wait_send()

    @pl.loop(1, 8)
    def _(d):
        c2((z + d) % 8, z).wait_send()


def spread(piece):
    D = pltpu.SemaphoreType.DMA
    return pl.pallas_call(
        spread_kernel,
        out_shape=jax.ShapeDtypeStruct((2, 16, 40, 128), jnp.float32),
        in_specs=[pl.BlockSpec(memory_space=pltpu.VMEM)],
        out_specs=pl.BlockSpec(memory_space=pltpu.VMEM),
        scratch_shapes=[
            pltpu.VMEM((16, 40, 128), jnp.float32),
            pltpu.VMEM((16, 40, 128), jnp.float32),
            pltpu.VMEM((16, 40, 128), jnp.float32),
            pltpu.VMEM((40, 128), jnp.float32),
            pltpu.VMEM((8, 40, 128), jnp.float32),
            D((16,)), D((16,)), D((16,)), D((16,)), D((8,)), D((8,)), D((16,)), D((16,)), D((16,)), D((16,)),
        ],
        compiler_params=pltpu.CompilerParams(collective_id=0, has_side_effects=True),
    )(piece)


def shards(ensemble, obs_x, obs_y, obs_level, owner_row, owner_col, obs_value, obs_noise, obs_var):
    cells = ensemble.reshape(MEMBERS, 32, 128)
    piece = pick(owner_row, owner_col, cells, obs_x, obs_y, obs_level)
    obs = spread(piece.reshape(2, 16, 40, 128)).reshape(2, 8, MEMBERS, 128)
    out = update(owner_row, owner_col, cells, obs, obs_x, obs_y, obs_level, obs_value, obs_noise, obs_var)
    return out.reshape(ensemble.shape)


def solution(mesh):
    in_specs = (P(None, None, "gx", "gy"), P(), P(), P(), P(), P(), P(), P(), P())
    out_specs = P(None, None, "gx", "gy")
    return jax.shard_map(shards, mesh=mesh, in_specs=in_specs, out_specs=out_specs, check_vma=False)
```

```python
import jax
import jax.numpy as jnp
from jax import lax
from jax.experimental import pallas as pl
from jax.experimental.pallas import tpu as pltpu
from jax.sharding import PartitionSpec as P

HIGH = lax.Precision.HIGHEST
F32 = jnp.float32
BF16 = jnp.bfloat16
LOC = 64
MEMBERS = 80
NT = (((1,), (1,)), ((), ()))
NN = (((1,), (0,)), ((), ()))


def split(v):
    hi = v.astype(BF16)
    lo = (v - hi.astype(F32)).astype(BF16)
    return hi, lo


def dot(a, b, dims=NN, precision=None):
    return lax.dot_general(a, b, dims, precision=precision, preferred_element_type=F32)


def pick_kernel(row_in, col_in, state, ox_in, oy_in, ol_in, out, row, col, ox, oy, ol, cells, sem, sem_cells):
    gx = lax.axis_index("gx")
    gy = lax.axis_index("gy")
    small = [(row_in, row), (col_in, col), (ox_in, ox), (oy_in, oy), (ol_in, ol)]
    small = [pltpu.make_async_copy(src, dst, sem.at[i]) for i, (src, dst) in enumerate(small)]
    for copy in small:
        copy.start()
    small[0].wait()
    small[1].wait()
    owned = [jnp.logical_and(row[b] == gx, col[b] == gy) for b in range(2)]

    @pl.when(jnp.logical_or(owned[0], owned[1]))
    def _():
        @pl.loop(0, 32)
        def _(r):
            pltpu.make_async_copy(state.at[:, r], cells.at[r], sem_cells).start()

    for copy in small[2:]:
        copy.wait()

    @pl.when(jnp.logical_or(owned[0], owned[1]))
    def _():
        pltpu.make_async_copy(cells, cells, sem_cells).wait()

    for b in range(2):

        @pl.when(owned[b])
        def _():
            @pl.loop(0, 8)
            def _(c):
                cols = pl.ds(pl.multiple_of(c * 128, 128), 128)
                want = jnp.broadcast_to(ol[b : b + 1, cols] * 8 + ox[b : b + 1, cols], (8, 128))
                at = jnp.broadcast_to(oy[b : b + 1, cols], (8, 128))
                for k in range(0, MEMBERS, 8):
                    got = jnp.zeros((8, 128), F32)
                    for r in range(32):
                        moved = jnp.take_along_axis(cells[r, k : k + 8], at, axis=1, mode="promise_in_bounds")
                        got = jnp.where(want == r, moved, got)
                    out[b, c, k : k + 8] = got

        @pl.when(jnp.logical_not(owned[b]))
        def _():
            out[b] = jnp.zeros((8, MEMBERS, 128), F32)


def inverse_of(a, keep):
    eye = jnp.where(
        lax.broadcasted_iota(jnp.int32, a.shape, 0) == lax.broadcasted_iota(jnp.int32, a.shape, 1), 1.0, 0.0
    )
    top = jnp.max(jnp.sum(jnp.abs(a), axis=1, keepdims=True), axis=0, keepdims=True)
    scale = 2.0 / (top + (MEMBERS - 1.0))
    r = eye - scale * a
    x = scale * (eye + r)
    for _ in range(5):
        r = dot(r, r, NN, HIGH)
        x = x + dot(x, r, NN, HIGH)

    keep[0] = x
    keep[1] = r

    def more(held):
        return jnp.logical_and(held[0] > 1e-4, held[1] < 40)

    def rest(held):
        r = dot(keep[1], keep[1], NN, HIGH)
        keep[0] = keep[0] + dot(keep[0], r, NN, HIGH)
        keep[1] = r
        return jnp.max(jnp.abs(r)), held[1] + 1

    _, count = lax.while_loop(more, rest, (jnp.max(jnp.abs(r)), jnp.int32(0)))

    @pl.when(count > 0)
    def _():
        x = keep[0]
        keep[0] = x + dot(x, eye - dot(a, x, NN, HIGH), NN, HIGH)

    return keep[0]


def update_kernel(row_in, col_in, state, obs, ox_in, oy_in, ol_in, value_in, noise_in, var_in, out,
                  row, col, ox, oy, ol, value, var, cells, hx, noises, both, scaled, cast, weights, near_y, col_x, col_y, col_f, taper, keep, gain_hi, gain_lo, passed,
                  sem_in, sem_obs, sem_out, sem_pass):
    gx = lax.axis_index("gx")
    gy = lax.axis_index("gy")
    small = [(row_in, row), (col_in, col), (ox_in, ox), (oy_in, oy), (ol_in, ol), (value_in, value), (var_in, var)]
    small += [(obs, hx), (noise_in, noises)]
    small = [pltpu.make_async_copy(src, dst, sem_obs.at[i]) for i, (src, dst) in enumerate(small)]
    for copy in small[:2]:
        copy.start()
    for copy in small[:2]:
        copy.wait()

    def close(b, x, y):
        return jnp.logical_and(jnp.abs(x - row[b]) <= 8, jnp.abs(y - col[b]) <= 1)

    near = [close(b, gx, gy) for b in range(2)]
    linked = jnp.logical_and(near[1], close(0, row[1], col[1]))
    any_near = jnp.logical_or(near[0], near[1])
    passing = [pl.ds(20 * i, 20) for i in range(4)]
    passing_in = [pltpu.make_async_copy(state.at[p], passed.at[p], sem_pass.at[i]) for i, p in enumerate(passing)]
    passing_out = [pltpu.make_async_copy(passed.at[p], out.at[p], sem_pass.at[i]) for i, p in enumerate(passing)]
    all_in = pltpu.make_async_copy(cells, cells, sem_in)
    all_out = pltpu.make_async_copy(cells, cells, sem_out)

    def fetch(r):
        return pltpu.make_async_copy(state.at[:, r], cells.at[r], sem_in)

    def store(r):
        return pltpu.make_async_copy(cells.at[r], out.at[:, r], sem_out)

    @pl.when(any_near)
    def _():
        for copy in small[2:]:
            copy.start()

        @pl.loop(0, 32)
        def _(r):
            fetch(r).start()

        for copy in small[2:]:
            copy.wait()

    @pl.when(jnp.logical_not(any_near))
    def _():
        for copy in passing_in:
            copy.start()
        for one, two in zip(passing_in, passing_out):
            one.wait()
            two.start()
        for copy in passing_out:
            copy.wait()

    def prepare(b):
        lane = lax.broadcasted_iota(jnp.int32, (1, 128), 1)
        mesh_y = (gy * 128 + lane - col[b] * 128).astype(F32) * (1.0 / LOC)

        @pl.loop(0, 8)
        def _(c):
            cols = pl.ds(pl.multiple_of(c * 128, 128), 128)
            h = hx[b, c]
            inv = 1.0 / var[b : b + 1, cols]
            o = h - jnp.sum(h, axis=0, keepdims=True) * (1.0 / MEMBERS)
            d = value[b : b + 1, cols] + noises[b, :, cols] - h
            both[0:MEMBERS, cols] = o
            both[MEMBERS : 2 * MEMBERS, cols] = d
            scaled[:, cols] = o * inv
            lev = ol[b : b + 1, cols].astype(F32)
            extra = [ox[b : b + 1, cols].astype(F32) * (1.0 / LOC), oy[b : b + 1, cols].astype(F32) * (1.0 / LOC)]
            for level in range(4):
                extra.append(1.0 / ((1.0 + jnp.abs(level - lev)) * (MEMBERS - 1)))
            extra.append(jnp.zeros((42, 128), F32))
            turned = jnp.concatenate([o] + extra, axis=0).T
            x_at = jnp.broadcast_to(turned[:, 80:81], (128, 128))
            y_at = jnp.broadcast_to(turned[:, 81:82], (128, 128))
            col_x[cols, :] = x_at
            col_y[cols, :] = y_at
            dy = mesh_y - y_at
            near_y[cols, :] = 1.0 - dy * dy
            turned_o = jnp.where(lane < MEMBERS, turned, 0.0)
            first = turned_o + jnp.where(lane >= MEMBERS, pltpu.roll(turned, MEMBERS, 1), 0.0)
            second = jnp.where(lane < 32, pltpu.roll(turned, MEMBERS, 1), 0.0) + pltpu.roll(turned_o, 32, 1)
            for level in range(5):
                if level < 4:
                    f_at = jnp.broadcast_to(turned[:, 82 + level : 83 + level], (128, 128))
                    col_f[level, cols, :] = f_at
                    left, right = first * f_at, second * f_at
                else:
                    left, right = first, second
                hi = right.astype(BF16).astype(F32)
                cast[level, cols, 0:128] = left.astype(BF16)
                cast[level, cols, 128:256] = jnp.where(lane < 32, hi, right - hi).astype(BF16)

        gram = dot(both[...], scaled[...], NT, HIGH)
        inner = gram[0:MEMBERS]
        eye = lax.broadcasted_iota(jnp.int32, (MEMBERS, MEMBERS), 0) == lax.broadcasted_iota(
            jnp.int32, (MEMBERS, MEMBERS), 1
        )
        trace = jnp.sum(jnp.sum(jnp.where(eye, inner, 0.0), axis=1, keepdims=True), axis=0, keepdims=True)
        inner = inner + jnp.where(eye, MEMBERS - 1.0, 0.0) + trace * (1.0 / MEMBERS / MEMBERS)
        inverse = inverse_of(inner, keep)
        factor = dot(gram[MEMBERS : 2 * MEMBERS], inverse, NN, HIGH)
        w = both[MEMBERS : 2 * MEMBERS] - dot(factor, both[0:MEMBERS], NN, HIGH)
        w = w * (1.0 / var[b : b + 1, :])
        hi, lo = split(w)
        weights[0:MEMBERS] = hi
        weights[MEMBERS : 2 * MEMBERS] = lo

    def spread_of(values):
        mean = jnp.sum(values, axis=0, keepdims=True) * (1.0 / MEMBERS)
        hi, lo = split(values - mean)
        return jnp.concatenate([hi, lo, hi, jnp.zeros((16, values.shape[1]), BF16)], axis=0)

    def gain(values, level, taper_at, slot=0):
        right = spread_of(values)
        wide = values.shape[1]
        for part in range(4):
            span = slice(part * 256, part * 256 + 256)
            cross = dot(cast[level, span, :], right)
            hi, lo = split(cross * taper_at(span))
            gain_hi[slot, span, 0:wide] = hi
            gain_lo[slot, span, 0:wide] = lo
        total = dot(weights[...], gain_hi[slot, :, 0:wide])
        rest = dot(weights[0:MEMBERS], gain_lo[slot, :, 0:wide])
        return total[0:MEMBERS] + total[MEMBERS : 2 * MEMBERS] + rest

    def move_state(b, last):
        @pl.loop(0, 4)
        def _(pair):
            for half in range(2):
                x = (gx * 8 + pair * 2 + half - row[b] * 8).astype(F32) * (1.0 / LOC)

                @pl.loop(0, 8)
                def _(c):
                    cols = pl.ds(pl.multiple_of(c * 128, 128), 128)
                    dx = x - col_x[cols, :]
                    t = jnp.maximum(near_y[cols, :] - dx * dx, 0.0)
                    taper[cols, half * 128 : half * 128 + 128] = t * t

            before = []
            for level in range(4):
                before.append([cells[level * 8 + pair * 2 + half] for half in range(2)])
            after = []
            for level in range(4):
                change = gain(jnp.concatenate(before[level], axis=1), level, lambda span: taper[span, :], level % 2)
                after.append([before[level][half] + change[:, half * 128 : half * 128 + 128] for half in range(2)])
            for level in range(4):
                for half in range(2):
                    cells[level * 8 + pair * 2 + half] = after[level][half]
            for level in range(4):
                for half in range(2):
                    r = level * 8 + pair * 2 + half
                    if last is True:
                        store(r).start()
                    else:
                        pl.when(last)(store(r).start)

    def move_obs():
        @pl.loop(0, 8)
        def _(c):
            cols = pl.ds(pl.multiple_of(c * 128, 128), 128)
            x = (ox[1:2, cols] + (row[1] - row[0]) * 8).astype(F32) * (1.0 / LOC)
            y = (oy[1:2, cols] + (col[1] - col[0]) * 128).astype(F32) * (1.0 / LOC)
            lev = ol[1:2, cols]

            def taper_at(span):
                dx = x - col_x[span, :]
                dy = y - col_y[span, :]
                t = jnp.maximum(1.0 - (dx * dx + dy * dy), 0.0)
                f = col_f[3, span, :]
                for level in range(3):
                    f = jnp.where(lev == level, col_f[level, span, :], f)
                return t * t * f

            h = hx[1, c]
            hx[1, c] = h + gain(h, 4, taper_at)

    @pl.when(jnp.logical_or(near[0], linked))
    def _():
        prepare(0)

    @pl.when(any_near)
    def _():
        all_in.wait()

    @pl.when(near[0])
    def _():
        move_state(0, jnp.logical_not(near[1]))

    @pl.when(linked)
    def _():
        move_obs()

    @pl.when(near[1])
    def _():
        prepare(1)
        move_state(1, True)

    @pl.when(any_near)
    def _():
        all_out.wait()


VMEM = pl.BlockSpec(memory_space=pltpu.VMEM)
SMEM = pl.BlockSpec(memory_space=pltpu.SMEM)
ANY = pl.BlockSpec(memory_space=pl.ANY)


def pick(row, col, state, ox, oy, ol):
    return pl.pallas_call(
        pick_kernel,
        out_shape=jax.ShapeDtypeStruct((2, 8, MEMBERS, 128), F32),
        in_specs=[ANY] * 6,
        out_specs=VMEM,
        scratch_shapes=[
            pltpu.SMEM((2,), jnp.int32),
            pltpu.SMEM((2,), jnp.int32),
            pltpu.VMEM((2, 1024), jnp.int32),
            pltpu.VMEM((2, 1024), jnp.int32),
            pltpu.VMEM((2, 1024), jnp.int32),
            pltpu.VMEM((32, MEMBERS, 128), F32),
            pltpu.SemaphoreType.DMA((5,)),
            pltpu.SemaphoreType.DMA,
        ],
        compiler_params=pltpu.CompilerParams(vmem_limit_bytes=60 * 2**20),
    )(row, col, state, ox, oy, ol)


def update(row, col, state, obs, ox, oy, ol, value, noise, var):
    S = pltpu.VMEM
    return pl.pallas_call(
        update_kernel,
        out_shape=jax.ShapeDtypeStruct(state.shape, F32),
        in_specs=[ANY] * 10,
        out_specs=ANY,
        scratch_shapes=[
            pltpu.SMEM((2,), jnp.int32),
            pltpu.SMEM((2,), jnp.int32),
            S((2, 1024), jnp.int32),
            S((2, 1024), jnp.int32),
            S((2, 1024), jnp.int32),
            S((2, 1024), F32),
            S((2, 1024), F32),
            S((32, MEMBERS, 128), F32),
            S((2, 8, MEMBERS, 128), F32),
            S((2, MEMBERS, 1024), F32),
            S((160, 1024), F32),
            S((MEMBERS, 1024), F32),
            S((5, 1024, 256), BF16),
            S((160, 1024), BF16),
            S((1024, 128), F32),
            S((1024, 128), F32),
            S((1024, 128), F32),
            S((4, 1024, 128), F32),
            S((1024, 256), F32),
            S((2, MEMBERS, MEMBERS), F32),
            S((2, 1024, 256), BF16),
            S((2, 1024, 256), BF16),
            S((MEMBERS, 32, 128), F32),
            pltpu.SemaphoreType.DMA,
            pltpu.SemaphoreType.DMA((9,)),
            pltpu.SemaphoreType.DMA,
            pltpu.SemaphoreType.DMA((4,)),
        ],
        compiler_params=pltpu.CompilerParams(vmem_limit_bytes=60 * 2**20),
    )(row, col, state, obs, ox, oy, ol, value, noise, var)


MESH = pl.DeviceIdType.MESH

def spread_kernel(piece, out, pair_buf, acc, ring_buf, z_src, z_buf,
                  s0s, s0r, s1s, s1r, s2s, s2r, s3s, s3r, s4s, s4r):
    gx = lax.axis_index("gx")
    gy = lax.axis_index("gy")
    yy = gx // 4
    zh = gx % 4
    zl = gy // 8
    xx = (gy // 2) % 4
    core = gy % 2
    other = 1 - core
    q = yy * 4 + xx
    z = zh * 2 + zl

    def dev_xy(t):
        return ((t // 4) * 4 + zh, zl * 8 + (t % 4) * 2 + core)

    def dev_z(t):
        return (yy * 4 + t // 2, (t % 2) * 8 + xx * 2 + core)

    mate = (gx, zl * 8 + xx * 2 + other)

    barrier = pltpu.get_barrier_semaphore()

    @pl.loop(1, 16)
    def _(d):
        pl.semaphore_signal(barrier, inc=1, device_id=dev_xy((q + d) % 16), device_id_type=MESH)

    @pl.loop(1, 8)
    def _(d):
        pl.semaphore_signal(barrier, inc=1, device_id=dev_z((z + d) % 8), device_id_type=MESH)

    pl.semaphore_signal(barrier, inc=1, device_id=mate, device_id_type=MESH)
    pl.semaphore_wait(barrier, 23)

    def c0(t):
        return pltpu.make_async_remote_copy(
            src_ref=piece.at[other, t], dst_ref=pair_buf.at[t], send_sem=s0s.at[t], recv_sem=s0r.at[t],
            device_id=mate, device_id_type=MESH)

    def c1(t, slot):
        return pltpu.make_async_remote_copy(
            src_ref=acc.at[t], dst_ref=ring_buf.at[slot], send_sem=s1s.at[t], recv_sem=s1r.at[slot],
            device_id=dev_xy(t), device_id_type=MESH)

    def c2(t, slot):
        return pltpu.make_async_remote_copy(
            src_ref=z_src, dst_ref=z_buf.at[slot], send_sem=s2s.at[t], recv_sem=s2r.at[slot],
            device_id=dev_z(t), device_id_type=MESH)

    def c3(t, slot):
        return pltpu.make_async_remote_copy(
            src_ref=out.at[core, slot], dst_ref=out.at[core, slot], send_sem=s3s.at[t], recv_sem=s3r.at[slot],
            device_id=dev_xy(t), device_id_type=MESH)

    def c4(w, slot):
        return pltpu.make_async_remote_copy(
            src_ref=out.at[w, slot], dst_ref=out.at[w, slot], send_sem=s4s.at[slot], recv_sem=s4r.at[slot],
            device_id=mate, device_id_type=MESH)

    @pl.loop(1, 17)
    def _(d):
        c0((q + d) % 16).start()

    @pl.loop(1, 16)
    def _(d):
        t = (q + d) % 16
        c0(t).wait_recv()
        acc[t] = piece[core, t] + pair_buf[t]
        c1(t, q).start()

    c0(q).wait_recv()
    z_src[...] = piece[core, q] + pair_buf[q]

    @pl.loop(1, 16)
    def _(d):
        t = (q + 16 - d) % 16
        c1(t, t).wait_recv()
        z_src[...] += ring_buf[t]

    @pl.loop(1, 8)
    def _(d):
        c2((z + d) % 8, z).start()

    out[core, q] = z_src[...]

    @pl.loop(1, 8)
    def _(d):
        t = (z + 8 - d) % 8
        c2(t, t).wait_recv()
        out[core, q] += z_buf[t]

    @pl.loop(1, 16)
    def _(d):
        c3((q + d) % 16, q).start()

    c4(core, q).start()

    @pl.loop(1, 16)
    def _(d):
        t = (q + 16 - d) % 16
        c3(t, t).wait_recv()
        c4(core, t).start()

    @pl.loop(0, 16)
    def _(d):
        c4(other, (q + 16 - d) % 16).wait_recv()

    @pl.loop(0, 16)
    def _(t):
        c0(t).wait_send()
        c4(core, t).wait_send()

    @pl.loop(1, 16)
    def _(d):
        t = (q + d) % 16
        c1(t, q).wait_send()
        c3(t, q).wait_send()

    @pl.loop(1, 8)
    def _(d):
        c2((z + d) % 8, z).wait_send()


def spread(piece):
    D = pltpu.SemaphoreType.DMA
    return pl.pallas_call(
        spread_kernel,
        out_shape=jax.ShapeDtypeStruct((2, 16, 40, 128), jnp.float32),
        in_specs=[pl.BlockSpec(memory_space=pltpu.VMEM)],
        out_specs=pl.BlockSpec(memory_space=pltpu.VMEM),
        scratch_shapes=[
            pltpu.VMEM((16, 40, 128), jnp.float32),
            pltpu.VMEM((16, 40, 128), jnp.float32),
            pltpu.VMEM((16, 40, 128), jnp.float32),
            pltpu.VMEM((40, 128), jnp.float32),
            pltpu.VMEM((8, 40, 128), jnp.float32),
            D((16,)), D((16,)), D((16,)), D((16,)), D((8,)), D((8,)), D((16,)), D((16,)), D((16,)), D((16,)),
        ],
        compiler_params=pltpu.CompilerParams(collective_id=0, has_side_effects=True),
    )(piece)


def shards(ensemble, obs_x, obs_y, obs_level, owner_row, owner_col, obs_value, obs_noise, obs_var):
    cells = ensemble.reshape(MEMBERS, 32, 128)
    piece = pick(owner_row, owner_col, cells, obs_x, obs_y, obs_level)
    obs = spread(piece.reshape(2, 16, 40, 128)).reshape(2, 8, MEMBERS, 128)
    out = update(owner_row, owner_col, cells, obs, obs_x, obs_y, obs_level, obs_value, obs_noise, obs_var)
    return out.reshape(ensemble.shape)


def solution(mesh):
    in_specs = (P(None, None, "gx", "gy"), P(), P(), P(), P(), P(), P(), P(), P())
    out_specs = P(None, None, "gx", "gy")
    return jax.shard_map(shards, mesh=mesh, in_specs=in_specs, out_specs=out_specs, check_vma=False)
```

```python
import jax
import jax.numpy as jnp
from jax import lax
from jax.experimental import pallas as pl
from jax.experimental.pallas import tpu as pltpu
from jax.sharding import PartitionSpec as P

HIGH = lax.Precision.HIGHEST
F32 = jnp.float32
BF16 = jnp.bfloat16
LOC = 64
MEMBERS = 80
NT = (((1,), (1,)), ((), ()))
NN = (((1,), (0,)), ((), ()))


def split(v):
    hi = v.astype(BF16)
    lo = (v - hi.astype(F32)).astype(BF16)
    return hi, lo


def dot(a, b, dims=NN, precision=None):
    return lax.dot_general(a, b, dims, precision=precision, preferred_element_type=F32)


def inverse_of(a, keep):
    eye = jnp.where(
        lax.broadcasted_iota(jnp.int32, a.shape, 0) == lax.broadcasted_iota(jnp.int32, a.shape, 1), 1.0, 0.0
    )
    top = jnp.max(jnp.sum(jnp.abs(a), axis=1, keepdims=True), axis=0, keepdims=True)
    scale = 2.0 / (top + (MEMBERS - 1.0))
    r = eye - scale * a
    x = scale * (eye + r)
    for _ in range(5):
        r = dot(r, r, NN, HIGH)
        x = x + dot(x, r, NN, HIGH)

    keep[0] = x
    keep[1] = r

    def more(held):
        return jnp.logical_and(held[0] > 1e-4, held[1] < 40)

    def rest(held):
        r = dot(keep[1], keep[1], NN, HIGH)
        keep[0] = keep[0] + dot(keep[0], r, NN, HIGH)
        keep[1] = r
        return jnp.max(jnp.abs(r)), held[1] + 1

    _, count = lax.while_loop(more, rest, (jnp.max(jnp.abs(r)), jnp.int32(0)))

    @pl.when(count > 0)
    def _():
        x = keep[0]
        keep[0] = x + dot(x, eye - dot(a, x, NN, HIGH), NN, HIGH)

    return keep[0]


def update_kernel(row_in, col_in, state, obs_in, ox_in, oy_in, ol_in, value_in, noise_in, var_in, out,
                  row, col, ox, oy, ol, value, var, obs, noises, cells, hx, both, scaled, cast, weights, near_y, col_x, col_y, col_f, taper, keep, gain_hi, gain_lo,
                  sem_in, sem_small, sem_out):
    gx = lax.axis_index("gx")
    gy = lax.axis_index("gy")
    small = [(row_in, row), (col_in, col), (ox_in, ox), (oy_in, oy), (ol_in, ol), (value_in, value), (var_in, var)]
    small += [(obs_in, obs), (noise_in, noises)]
    small = [pltpu.make_async_copy(src, dst, sem_small.at[i]) for i, (src, dst) in enumerate(small)]
    for copy in small:
        copy.start()

    def fetch(r):
        return pltpu.make_async_copy(state.at[:, r], cells.at[r], sem_in)

    def store(r):
        return pltpu.make_async_copy(cells.at[r], out.at[:, r], sem_out)

    @pl.loop(0, 32)
    def _(r):
        fetch(r).start()

    for copy in small[:2]:
        copy.wait()

    def close(b, x, y):
        return jnp.logical_and(jnp.abs(x - row[b]) <= 8, jnp.abs(y - col[b]) <= 1)

    near = [close(b, gx, gy) for b in range(2)]
    linked = jnp.logical_and(near[1], close(0, row[1], col[1]))
    any_near = jnp.logical_or(near[0], near[1])
    all_in = pltpu.make_async_copy(cells, cells, sem_in)
    all_out = pltpu.make_async_copy(cells, cells, sem_out)

    for copy in small[2:]:
        copy.wait()

    @pl.when(linked)
    def _():
        hx[...] = obs[1]

    def members_of(ref, c):
        return jnp.concatenate([ref[2 * c + j] for j in range(2)], axis=0)

    def prepare(b, source):
        lane = lax.broadcasted_iota(jnp.int32, (1, 128), 1)
        mesh_y = (gy * 128 + lane - col[b] * 128).astype(F32) * (1.0 / LOC)

        @pl.loop(0, 8)
        def _(c):
            cols = pl.ds(pl.multiple_of(c * 128, 128), 128)
            h = members_of(source, c)
            inv = 1.0 / var[b : b + 1, cols]
            o = h - jnp.sum(h, axis=0, keepdims=True) * (1.0 / MEMBERS)
            d = value[b : b + 1, cols] + noises[b, :, cols] - h
            both[0:MEMBERS, cols] = o
            both[MEMBERS : 2 * MEMBERS, cols] = d
            scaled[:, cols] = o * inv
            lev = ol[b : b + 1, cols].astype(F32)
            extra = [ox[b : b + 1, cols].astype(F32) * (1.0 / LOC), oy[b : b + 1, cols].astype(F32) * (1.0 / LOC)]
            for level in range(4):
                extra.append(1.0 / ((1.0 + jnp.abs(level - lev)) * (MEMBERS - 1)))
            extra.append(jnp.zeros((42, 128), F32))
            turned = jnp.concatenate([o] + extra, axis=0).T
            x_at = jnp.broadcast_to(turned[:, 80:81], (128, 128))
            y_at = jnp.broadcast_to(turned[:, 81:82], (128, 128))
            col_x[cols, :] = x_at
            col_y[cols, :] = y_at
            dy = mesh_y - y_at
            near_y[cols, :] = 1.0 - dy * dy
            turned_o = jnp.where(lane < MEMBERS, turned, 0.0)
            first = turned_o + jnp.where(lane >= MEMBERS, pltpu.roll(turned, MEMBERS, 1), 0.0)
            second = jnp.where(lane < 32, pltpu.roll(turned, MEMBERS, 1), 0.0) + pltpu.roll(turned_o, 32, 1)
            for level in range(5):
                if level < 4:
                    f_at = jnp.broadcast_to(turned[:, 82 + level : 83 + level], (128, 128))
                    col_f[level, cols, :] = f_at
                    left, right = first * f_at, second * f_at
                else:
                    left, right = first, second
                hi = right.astype(BF16).astype(F32)
                cast[level, cols, 0:128] = left.astype(BF16)
                cast[level, cols, 128:256] = jnp.where(lane < 32, hi, right - hi).astype(BF16)

        gram = dot(both[...], scaled[...], NT, HIGH)
        inner = gram[0:MEMBERS]
        eye = lax.broadcasted_iota(jnp.int32, (MEMBERS, MEMBERS), 0) == lax.broadcasted_iota(
            jnp.int32, (MEMBERS, MEMBERS), 1
        )
        trace = jnp.sum(jnp.sum(jnp.where(eye, inner, 0.0), axis=1, keepdims=True), axis=0, keepdims=True)
        inner = inner + jnp.where(eye, MEMBERS - 1.0, 0.0) + trace * (1.0 / MEMBERS / MEMBERS)
        inverse = inverse_of(inner, keep)
        factor = dot(gram[MEMBERS : 2 * MEMBERS], inverse, NN, HIGH)
        w = both[MEMBERS : 2 * MEMBERS] - dot(factor, both[0:MEMBERS], NN, HIGH)
        w = w * (1.0 / var[b : b + 1, :])
        hi, lo = split(w)
        weights[0:MEMBERS] = hi
        weights[MEMBERS : 2 * MEMBERS] = lo

    def spread_of(values):
        mean = jnp.sum(values, axis=0, keepdims=True) * (1.0 / MEMBERS)
        hi, lo = split(values - mean)
        return jnp.concatenate([hi, lo, hi, jnp.zeros((16, values.shape[1]), BF16)], axis=0)

    def gain(values, level, taper_at, slot=0):
        right = spread_of(values)
        wide = values.shape[1]
        for part in range(4):
            span = slice(part * 256, part * 256 + 256)
            cross = dot(cast[level, span, :], right)
            hi, lo = split(cross * taper_at(span))
            gain_hi[slot, span, 0:wide] = hi
            gain_lo[slot, span, 0:wide] = lo
        total = dot(weights[...], gain_hi[slot, :, 0:wide])
        rest = dot(weights[0:MEMBERS], gain_lo[slot, :, 0:wide])
        return total[0:MEMBERS] + total[MEMBERS : 2 * MEMBERS] + rest

    def move_state(b, last):
        @pl.loop(0, 4)
        def _(pair):
            for half in range(2):
                x = (gx * 8 + pair * 2 + half - row[b] * 8).astype(F32) * (1.0 / LOC)

                @pl.loop(0, 8)
                def _(c):
                    cols = pl.ds(pl.multiple_of(c * 128, 128), 128)
                    dx = x - col_x[cols, :]
                    t = jnp.maximum(near_y[cols, :] - dx * dx, 0.0)
                    taper[cols, half * 128 : half * 128 + 128] = t * t

            before = []
            for level in range(4):
                before.append([cells[level * 8 + pair * 2 + half] for half in range(2)])
            after = []
            for level in range(4):
                change = gain(jnp.concatenate(before[level], axis=1), level, lambda span: taper[span, :], level % 2)
                after.append([before[level][half] + change[:, half * 128 : half * 128 + 128] for half in range(2)])
            for level in range(4):
                for half in range(2):
                    cells[level * 8 + pair * 2 + half] = after[level][half]
            for level in range(4):
                for half in range(2):
                    r = level * 8 + pair * 2 + half
                    if last is True:
                        store(r).start()
                    else:
                        pl.when(last)(store(r).start)

    def move_obs():
        @pl.loop(0, 8)
        def _(c):
            cols = pl.ds(pl.multiple_of(c * 128, 128), 128)
            x = (ox[1:2, cols] + (row[1] - row[0]) * 8).astype(F32) * (1.0 / LOC)
            y = (oy[1:2, cols] + (col[1] - col[0]) * 128).astype(F32) * (1.0 / LOC)
            lev = ol[1:2, cols]

            def taper_at(span):
                dx = x - col_x[span, :]
                dy = y - col_y[span, :]
                t = jnp.maximum(1.0 - (dx * dx + dy * dy), 0.0)
                f = col_f[3, span, :]
                for level in range(3):
                    f = jnp.where(lev == level, col_f[level, span, :], f)
                return t * t * f

            h = members_of(hx, c)
            h = h + gain(h, 4, taper_at)
            for j in range(2):
                hx[2 * c + j] = h[40 * j : 40 * j + 40]

    @pl.when(jnp.logical_or(near[0], linked))
    def _():
        prepare(0, obs.at[0])

    all_in.wait()

    @pl.when(jnp.logical_not(any_near))
    def _():
        @pl.loop(0, 32)
        def _(r):
            store(r).start()

    @pl.when(near[0])
    def _():
        move_state(0, jnp.logical_not(near[1]))

    @pl.when(linked)
    def _():
        move_obs()

    @pl.when(near[1])
    def _():
        @pl.when(jnp.logical_not(linked))
        def _():
            hx[...] = obs[1]

        prepare(1, hx)
        move_state(1, True)

    all_out.wait()


VMEM = pl.BlockSpec(memory_space=pltpu.VMEM)
SMEM = pl.BlockSpec(memory_space=pltpu.SMEM)
ANY = pl.BlockSpec(memory_space=pl.ANY)


def update(row, col, state, obs, ox, oy, ol, value, noise, var):
    S = pltpu.VMEM
    return pl.pallas_call(
        update_kernel,
        out_shape=jax.ShapeDtypeStruct(state.shape, F32),
        in_specs=[ANY] * 10,
        out_specs=ANY,
        scratch_shapes=[
            pltpu.SMEM((2,), jnp.int32),
            pltpu.SMEM((2,), jnp.int32),
            S((2, 1024), jnp.int32),
            S((2, 1024), jnp.int32),
            S((2, 1024), jnp.int32),
            S((2, 1024), F32),
            S((2, 1024), F32),
            S((2, 16, 40, 128), F32),
            S((2, MEMBERS, 1024), F32),
            S((32, MEMBERS, 128), F32),
            S((16, 40, 128), F32),
            S((160, 1024), F32),
            S((MEMBERS, 1024), F32),
            S((5, 1024, 256), BF16),
            S((160, 1024), BF16),
            S((1024, 128), F32),
            S((1024, 128), F32),
            S((1024, 128), F32),
            S((4, 1024, 128), F32),
            S((1024, 256), F32),
            S((2, MEMBERS, MEMBERS), F32),
            S((2, 1024, 256), BF16),
            S((2, 1024, 256), BF16),
            pltpu.SemaphoreType.DMA,
            pltpu.SemaphoreType.DMA((9,)),
            pltpu.SemaphoreType.DMA,
        ],
        compiler_params=pltpu.CompilerParams(vmem_limit_bytes=60 * 2**20),
    )(row, col, state, obs, ox, oy, ol, value, noise, var)


MESH = pl.DeviceIdType.MESH


FAR = sorted(((dx, dy) for dx in range(4) for dy in range(4) if dx or dy), key=lambda o: -sum(min(d, 4 - d) for d in o))


def spread_kernel(row_in, col_in, state, ox_in, oy_in, ol_in, out,
                  row, col, ox, oy, ol, cells, piece, pair_buf, acc, ring_buf, z_src, z_buf,
                  sem, sem_cells, s0s, s0r, s1s, s1r, s2s, s2r, s3s, s3r, s4s, s4r):
    gx = lax.axis_index("gx")
    gy = lax.axis_index("gy")
    yy = gx // 4
    zh = gx % 4
    zl = gy // 8
    xx = (gy // 2) % 4
    core = gy % 2
    other = 1 - core
    q = yy * 4 + xx
    z = zh * 2 + zl

    def dev_xy(t):
        return ((t // 4) * 4 + zh, zl * 8 + (t % 4) * 2 + core)

    def dev_z(t):
        return (yy * 4 + t // 2, (t % 2) * 8 + xx * 2 + core)

    mate = (gx, zl * 8 + xx * 2 + other)
    ahead = [((yy + dy) % 4) * 4 + (xx + dx) % 4 for dx, dy in FAR]
    behind = [((yy + 4 - dy) % 4) * 4 + (xx + 4 - dx) % 4 for dx, dy in reversed(FAR)]

    small = [(row_in, row), (col_in, col), (ox_in, ox), (oy_in, oy), (ol_in, ol)]
    small = [pltpu.make_async_copy(src, dst, sem.at[i]) for i, (src, dst) in enumerate(small)]
    for copy in small:
        copy.start()

    @pl.loop(0, 32)
    def _(r):
        pltpu.make_async_copy(state.at[:, r], cells.at[r], sem_cells).start()

    barrier = pltpu.get_barrier_semaphore()

    @pl.loop(1, 16)
    def _(d):
        pl.semaphore_signal(barrier, inc=1, device_id=dev_xy((q + d) % 16), device_id_type=MESH)

    @pl.loop(1, 8)
    def _(d):
        pl.semaphore_signal(barrier, inc=1, device_id=dev_z((z + d) % 8), device_id_type=MESH)

    pl.semaphore_signal(barrier, inc=1, device_id=mate, device_id_type=MESH)

    for copy in small:
        copy.wait()
    pltpu.make_async_copy(cells, cells, sem_cells).wait()

    def gather(b, g):
        cols = pl.ds(pl.multiple_of(g * 128, 128), 128)
        mine = jnp.logical_and(row[b] == gx, col[b] == gy).astype(F32)
        want = ol[:, cols] * 8 + ox[:, cols]
        want = jnp.broadcast_to(jnp.where(b == 0, want[0:1], want[1:2]), (8, 128))
        at = oy[:, cols]
        at = jnp.broadcast_to(jnp.where(b == 0, at[0:1], at[1:2]), (8, 128))
        for k in range(0, MEMBERS, 8):
            got = jnp.zeros((8, 128), F32)
            for r in range(32):
                moved = jnp.take_along_axis(cells[r, k : k + 8], at, axis=1, mode="promise_in_bounds")
                got = jnp.where(want == r, moved, got)
            piece[b, 2 * g + k // 40, k % 40 : k % 40 + 8] = got * mine

    def remote(src, dst, send, recv, to):
        return pltpu.make_async_remote_copy(
            src_ref=src, dst_ref=dst, send_sem=send, recv_sem=recv, device_id=to, device_id_type=MESH)

    def c0(g):
        two = pl.ds(2 * g, 2)
        return remote(piece.at[other, two], pair_buf.at[two], s0s.at[g], s0r.at[g], mate)

    def c1(t, slot):
        return remote(acc.at[t], ring_buf.at[slot], s1s.at[t], s1r.at[slot], dev_xy(t))

    def c2(t, slot):
        return remote(z_src, z_buf.at[slot], s2s.at[t], s2r.at[slot], dev_z(t))

    def c3(t, slot):
        return remote(out.at[core, slot], out.at[core, slot], s3s.at[t], s3r.at[slot], dev_xy(t))

    def c4(b, slot):
        return remote(out.at[b, slot], out.at[b, slot], s4s.at[slot], s4r.at[slot], mate)

    pl.semaphore_wait(barrier, 23)

    @pl.loop(0, 8)
    def _(i):
        g = (q // 2 + 1 + i) % 8
        gather(other, g)
        c0(g).start()

    @pl.loop(0, 8)
    def _(i):
        g = (q // 2 + 1 + i) % 8
        gather(core, g)
        c0(g).wait_recv()
        for j in range(2):
            t = 2 * g + j
            acc[t] = piece[core, t] + pair_buf[t]

            @pl.when(t != q)
            def _():
                c1(t, q).start()

    total = acc[q]
    for t in behind:
        c1(t, t).wait_recv()
        total = total + ring_buf[t]
    z_src[...] = total
    for d in (4, 3, 5, 2, 6, 1, 7):
        c2((z + d) % 8, z).start()
    for d in (1, 7, 2, 6, 3, 5, 4):
        t = (z + 8 - d) % 8
        c2(t, t).wait_recv()
        total = total + z_buf[t]
    out[core, q] = total
    for t in ahead:
        c3(t, q).start()
    c4(core, q).start()
    for t in behind:
        c3(t, t).wait_recv()
        c4(core, t).start()

    @pl.loop(0, 16)
    def _(t):
        c4(other, t).wait_recv()

    @pl.loop(0, 8)
    def _(g):
        c0(g).wait_send()

    @pl.loop(0, 16)
    def _(t):
        c4(core, t).wait_send()

    @pl.loop(1, 16)
    def _(d):
        t = (q + d) % 16
        c1(t, q).wait_send()
        c3(t, q).wait_send()

    @pl.loop(1, 8)
    def _(d):
        c2((z + d) % 8, z).wait_send()


def spread(row, col, state, ox, oy, ol):
    D = pltpu.SemaphoreType.DMA
    S = pltpu.VMEM
    return pl.pallas_call(
        spread_kernel,
        out_shape=jax.ShapeDtypeStruct((2, 16, 40, 128), F32),
        in_specs=[ANY] * 6,
        out_specs=VMEM,
        scratch_shapes=[
            pltpu.SMEM((2,), jnp.int32),
            pltpu.SMEM((2,), jnp.int32),
            S((2, 1024), jnp.int32),
            S((2, 1024), jnp.int32),
            S((2, 1024), jnp.int32),
            S((32, MEMBERS, 128), F32),
            S((2, 16, 40, 128), F32),
            S((16, 40, 128), F32),
            S((16, 40, 128), F32),
            S((16, 40, 128), F32),
            S((40, 128), F32),
            S((8, 40, 128), F32),
            D((5,)), D,
            D((8,)), D((8,)), D((16,)), D((16,)), D((8,)), D((8,)), D((16,)), D((16,)), D((16,)), D((16,)),
        ],
        compiler_params=pltpu.CompilerParams(
            collective_id=0, has_side_effects=True, vmem_limit_bytes=60 * 2**20),
    )(row, col, state, ox, oy, ol)


def shards(ensemble, obs_x, obs_y, obs_level, owner_row, owner_col, obs_value, obs_noise, obs_var):
    cells = ensemble.reshape(MEMBERS, 32, 128)
    obs = spread(owner_row, owner_col, cells, obs_x, obs_y, obs_level)
    out = update(owner_row, owner_col, cells, obs, obs_x, obs_y, obs_level, obs_value, obs_noise, obs_var)
    return out.reshape(ensemble.shape)


def solution(mesh):
    in_specs = (P(None, None, "gx", "gy"), P(), P(), P(), P(), P(), P(), P(), P())
    out_specs = P(None, None, "gx", "gy")
    return jax.shard_map(shards, mesh=mesh, in_specs=in_specs, out_specs=out_specs, check_vma=False)
```

```python
import jax
import jax.numpy as jnp
from jax import lax
from jax.experimental import pallas as pl
from jax.experimental.pallas import tpu as pltpu
from jax.sharding import PartitionSpec as P

HIGH = lax.Precision.HIGHEST
F32 = jnp.float32
BF16 = jnp.bfloat16
LOC = 64
MEMBERS = 80
NT = (((1,), (1,)), ((), ()))
NN = (((1,), (0,)), ((), ()))


def split(v):
    hi = v.astype(BF16)
    lo = (v - hi.astype(F32)).astype(BF16)
    return hi, lo


def dot(a, b, dims=NN, precision=None):
    return lax.dot_general(a, b, dims, precision=precision, preferred_element_type=F32)


def inverse_of(a, keep):
    eye = jnp.where(
        lax.broadcasted_iota(jnp.int32, a.shape, 0) == lax.broadcasted_iota(jnp.int32, a.shape, 1), 1.0, 0.0
    )
    top = jnp.max(jnp.sum(jnp.abs(a), axis=1, keepdims=True), axis=0, keepdims=True)
    scale = 2.0 / (top + (MEMBERS - 1.0))
    r = eye - scale * a
    x = scale * (eye + r)
    for _ in range(5):
        r = dot(r, r, NN, HIGH)
        x = x + dot(x, r, NN, HIGH)

    keep[0] = x
    keep[1] = r

    def more(held):
        return jnp.logical_and(held[0] > 1e-4, held[1] < 40)

    def rest(held):
        r = dot(keep[1], keep[1], NN, HIGH)
        keep[0] = keep[0] + dot(keep[0], r, NN, HIGH)
        keep[1] = r
        return jnp.max(jnp.abs(r)), held[1] + 1

    _, count = lax.while_loop(more, rest, (jnp.max(jnp.abs(r)), jnp.int32(0)))

    @pl.when(count > 0)
    def _():
        x = keep[0]
        keep[0] = x + dot(x, eye - dot(a, x, NN, HIGH), NN, HIGH)

    return keep[0]


def update_kernel(row_in, col_in, state, obs_in, ox_in, oy_in, ol_in, value_in, noise_in, var_in, out,
                  row, col, ox, oy, ol, value, var, obs, noises, cells, hx, both, scaled, cast, weights, near_y, col_x, col_y, col_f, taper, keep, gain_hi, gain_lo,
                  sem_in, sem_small, sem_out):
    gx = lax.axis_index("gx")
    gy = lax.axis_index("gy")
    small = [(row_in, row), (col_in, col), (ox_in, ox), (oy_in, oy), (ol_in, ol), (value_in, value), (var_in, var)]
    small += [(obs_in, obs), (noise_in, noises)]
    small = [pltpu.make_async_copy(src, dst, sem_small.at[i]) for i, (src, dst) in enumerate(small)]
    for copy in small:
        copy.start()

    def fetch(r):
        return pltpu.make_async_copy(state.at[:, r], cells.at[r], sem_in)

    def store(r):
        return pltpu.make_async_copy(cells.at[r], out.at[:, r], sem_out)

    @pl.loop(0, 32)
    def _(r):
        fetch(r).start()

    for copy in small[:2]:
        copy.wait()

    def close(b, x, y):
        return jnp.logical_and(jnp.abs(x - row[b]) <= 8, jnp.abs(y - col[b]) <= 1)

    near = [close(b, gx, gy) for b in range(2)]
    linked = jnp.logical_and(near[1], close(0, row[1], col[1]))
    any_near = jnp.logical_or(near[0], near[1])
    all_in = pltpu.make_async_copy(cells, cells, sem_in)
    all_out = pltpu.make_async_copy(cells, cells, sem_out)

    for copy in small[2:]:
        copy.wait()

    @pl.when(linked)
    def _():
        hx[...] = obs[1]

    def members_of(ref, c):
        return jnp.concatenate([ref[2 * c + j] for j in range(2)], axis=0)

    def prepare(b, source):
        lane = lax.broadcasted_iota(jnp.int32, (1, 128), 1)
        mesh_y = (gy * 128 + lane - col[b] * 128).astype(F32) * (1.0 / LOC)

        @pl.loop(0, 8)
        def _(c):
            cols = pl.ds(pl.multiple_of(c * 128, 128), 128)
            h = members_of(source, c)
            inv = 1.0 / var[b : b + 1, cols]
            o = h - jnp.sum(h, axis=0, keepdims=True) * (1.0 / MEMBERS)
            d = value[b : b + 1, cols] + noises[b, :, cols] - h
            both[0:MEMBERS, cols] = o
            both[MEMBERS : 2 * MEMBERS, cols] = d
            scaled[:, cols] = o * inv
            lev = ol[b : b + 1, cols].astype(F32)
            extra = [ox[b : b + 1, cols].astype(F32) * (1.0 / LOC), oy[b : b + 1, cols].astype(F32) * (1.0 / LOC)]
            for level in range(4):
                extra.append(1.0 / ((1.0 + jnp.abs(level - lev)) * (MEMBERS - 1)))
            extra.append(jnp.zeros((42, 128), F32))
            turned = jnp.concatenate([o] + extra, axis=0).T
            x_at = jnp.broadcast_to(turned[:, 80:81], (128, 128))
            y_at = jnp.broadcast_to(turned[:, 81:82], (128, 128))
            col_x[cols, :] = x_at
            col_y[cols, :] = y_at
            dy = mesh_y - y_at
            near_y[cols, :] = 1.0 - dy * dy
            turned_o = jnp.where(lane < MEMBERS, turned, 0.0)
            first = turned_o + jnp.where(lane >= MEMBERS, pltpu.roll(turned, MEMBERS, 1), 0.0)
            second = jnp.where(lane < 32, pltpu.roll(turned, MEMBERS, 1), 0.0) + pltpu.roll(turned_o, 32, 1)
            for level in range(5):
                if level < 4:
                    f_at = jnp.broadcast_to(turned[:, 82 + level : 83 + level], (128, 128))
                    col_f[level, cols, :] = f_at
                    left, right = first * f_at, second * f_at
                else:
                    left, right = first, second
                hi = right.astype(BF16).astype(F32)
                cast[level, cols, 0:128] = left.astype(BF16)
                cast[level, cols, 128:256] = jnp.where(lane < 32, hi, right - hi).astype(BF16)

        gram = dot(both[...], scaled[...], NT, HIGH)
        inner = gram[0:MEMBERS]
        eye = lax.broadcasted_iota(jnp.int32, (MEMBERS, MEMBERS), 0) == lax.broadcasted_iota(
            jnp.int32, (MEMBERS, MEMBERS), 1
        )
        trace = jnp.sum(jnp.sum(jnp.where(eye, inner, 0.0), axis=1, keepdims=True), axis=0, keepdims=True)
        inner = inner + jnp.where(eye, MEMBERS - 1.0, 0.0) + trace * (1.0 / MEMBERS / MEMBERS)
        inverse = inverse_of(inner, keep)
        factor = dot(gram[MEMBERS : 2 * MEMBERS], inverse, NN, HIGH)
        w = both[MEMBERS : 2 * MEMBERS] - dot(factor, both[0:MEMBERS], NN, HIGH)
        w = w * (1.0 / var[b : b + 1, :])
        hi, lo = split(w)
        weights[0:MEMBERS] = hi
        weights[MEMBERS : 2 * MEMBERS] = lo

    def spread_of(values):
        mean = jnp.sum(values, axis=0, keepdims=True) * (1.0 / MEMBERS)
        hi, lo = split(values - mean)
        return jnp.concatenate([hi, lo, hi, jnp.zeros((16, values.shape[1]), BF16)], axis=0)

    def gain(values, level, taper_at, slot=0):
        right = spread_of(values)
        wide = values.shape[1]
        for part in range(2):
            span = slice(part * 512, part * 512 + 512)
            cross = dot(cast[level, span, :], right)
            hi, lo = split(cross * taper_at(span))
            gain_hi[slot, span, 0:wide] = hi
            gain_lo[slot, span, 0:wide] = lo
        total = dot(weights[...], gain_hi[slot, :, 0:wide])
        rest = dot(weights[0:MEMBERS], gain_lo[slot, :, 0:wide])
        return total[0:MEMBERS] + total[MEMBERS : 2 * MEMBERS] + rest

    def move_state(b, last):
        @pl.loop(0, 4)
        def _(pair):
            x = [(gx * 8 + pair * 2 + half - row[b] * 8).astype(F32) * (1.0 / LOC) for half in range(2)]

            def taper_at(span):
                parts = []
                for half in range(2):
                    dx = x[half] - col_x[span, :]
                    t = jnp.maximum(near_y[span, :] - dx * dx, 0.0)
                    parts.append(t * t)
                t = jnp.concatenate(parts, axis=1)
                taper[span, :] = t
                return t

            before = []
            for level in range(4):
                before.append([cells[level * 8 + pair * 2 + half] for half in range(2)])
            after = []
            for level in range(4):
                change = gain(jnp.concatenate(before[level], axis=1), level, (lambda span: taper[span, :]) if level else taper_at, level % 2)
                after.append([before[level][half] + change[:, half * 128 : half * 128 + 128] for half in range(2)])
            for level in range(4):
                for half in range(2):
                    cells[level * 8 + pair * 2 + half] = after[level][half]
            for level in range(4):
                for half in range(2):
                    r = level * 8 + pair * 2 + half
                    if last is True:
                        store(r).start()
                    else:
                        pl.when(last)(store(r).start)

    def move_obs():
        @pl.loop(0, 4)
        def _(c):
            cols = pl.ds(pl.multiple_of(c * 256, 256), 256)
            x = (ox[1:2, cols] + (row[1] - row[0]) * 8).astype(F32) * (1.0 / LOC)
            y = (oy[1:2, cols] + (col[1] - col[0]) * 128).astype(F32) * (1.0 / LOC)
            lev = ol[1:2, cols]
            at = [lev == level for level in range(3)]

            def taper_at(span):
                parts = []
                for half in range(2):
                    here = slice(half * 128, half * 128 + 128)
                    dx = x[:, here] - col_x[span, :]
                    dy = y[:, here] - col_y[span, :]
                    t = jnp.maximum(1.0 - (dx * dx + dy * dy), 0.0)
                    f = col_f[3, span, :]
                    for level in range(3):
                        f = jnp.where(at[level][:, here], col_f[level, span, :], f)
                    parts.append(t * t * f)
                return jnp.concatenate(parts, axis=1)

            h = jnp.concatenate([members_of(hx, 2 * c + half) for half in range(2)], axis=1)
            h = h + gain(h, 4, taper_at)
            for j in range(4):
                hx[4 * c + j] = h[40 * (j % 2) : 40 * (j % 2) + 40, 128 * (j // 2) : 128 * (j // 2) + 128]

    @pl.when(jnp.logical_or(near[0], linked))
    def _():
        prepare(0, obs.at[0])

    all_in.wait()

    @pl.when(jnp.logical_not(any_near))
    def _():
        @pl.loop(0, 32)
        def _(r):
            store(r).start()

    @pl.when(near[0])
    def _():
        move_state(0, jnp.logical_not(near[1]))

    @pl.when(linked)
    def _():
        move_obs()

    @pl.when(near[1])
    def _():
        @pl.when(jnp.logical_not(linked))
        def _():
            hx[...] = obs[1]

        prepare(1, hx)
        move_state(1, True)

    all_out.wait()


VMEM = pl.BlockSpec(memory_space=pltpu.VMEM)
SMEM = pl.BlockSpec(memory_space=pltpu.SMEM)
ANY = pl.BlockSpec(memory_space=pl.ANY)


def update(row, col, state, obs, ox, oy, ol, value, noise, var):
    S = pltpu.VMEM
    return pl.pallas_call(
        update_kernel,
        out_shape=jax.ShapeDtypeStruct(state.shape, F32),
        in_specs=[ANY] * 10,
        out_specs=ANY,
        scratch_shapes=[
            pltpu.SMEM((2,), jnp.int32),
            pltpu.SMEM((2,), jnp.int32),
            S((2, 1024), jnp.int32),
            S((2, 1024), jnp.int32),
            S((2, 1024), jnp.int32),
            S((2, 1024), F32),
            S((2, 1024), F32),
            S((2, 16, 40, 128), F32),
            S((2, MEMBERS, 1024), F32),
            S((32, MEMBERS, 128), F32),
            S((16, 40, 128), F32),
            S((160, 1024), F32),
            S((MEMBERS, 1024), F32),
            S((5, 1024, 256), BF16),
            S((160, 1024), BF16),
            S((1024, 128), F32),
            S((1024, 128), F32),
            S((1024, 128), F32),
            S((4, 1024, 128), F32),
            S((1024, 256), F32),
            S((2, MEMBERS, MEMBERS), F32),
            S((2, 1024, 256), BF16),
            S((2, 1024, 256), BF16),
            pltpu.SemaphoreType.DMA,
            pltpu.SemaphoreType.DMA((9,)),
            pltpu.SemaphoreType.DMA,
        ],
        compiler_params=pltpu.CompilerParams(vmem_limit_bytes=60 * 2**20),
    )(row, col, state, obs, ox, oy, ol, value, noise, var)


MESH = pl.DeviceIdType.MESH


FAR = sorted(((dx, dy) for dx in range(4) for dy in range(4) if dx or dy), key=lambda o: -sum(min(d, 4 - d) for d in o))


def spread_kernel(row_in, col_in, state, ox_in, oy_in, ol_in, out,
                  row, col, ox, oy, ol, cells, piece, pair_buf, acc, ring_buf, z_src, z_buf, full,
                  sem, sem_cells, sem_out, s0s, s0r, s1s, s1r, s2s, s2r, s3s, s3r, s4s, s4r):
    gx = lax.axis_index("gx")
    gy = lax.axis_index("gy")
    yy = gx // 4
    zh = gx % 4
    zl = gy // 8
    xx = (gy // 2) % 4
    core = gy % 2
    other = 1 - core
    q = yy * 4 + xx
    z = zh * 2 + zl

    def dev_xy(t):
        return ((t // 4) * 4 + zh, zl * 8 + (t % 4) * 2 + core)

    def dev_z(t):
        return (yy * 4 + t // 2, (t % 2) * 8 + xx * 2 + core)

    mate = (gx, zl * 8 + xx * 2 + other)
    ahead = [((yy + dy) % 4) * 4 + (xx + dx) % 4 for dx, dy in FAR]
    behind = [((yy + 4 - dy) % 4) * 4 + (xx + 4 - dx) % 4 for dx, dy in reversed(FAR)]

    small = [(row_in, row), (col_in, col), (ox_in, ox), (oy_in, oy), (ol_in, ol)]
    small = [pltpu.make_async_copy(src, dst, sem.at[i]) for i, (src, dst) in enumerate(small)]
    for copy in small:
        copy.start()

    @pl.loop(0, 32)
    def _(r):
        pltpu.make_async_copy(state.at[:, r], cells.at[r], sem_cells).start()

    barrier = pltpu.get_barrier_semaphore()

    @pl.loop(1, 16)
    def _(d):
        pl.semaphore_signal(barrier, inc=1, device_id=dev_xy((q + d) % 16), device_id_type=MESH)

    @pl.loop(1, 8)
    def _(d):
        pl.semaphore_signal(barrier, inc=1, device_id=dev_z((z + d) % 8), device_id_type=MESH)

    pl.semaphore_signal(barrier, inc=1, device_id=mate, device_id_type=MESH)

    for copy in small:
        copy.wait()
    pltpu.make_async_copy(cells, cells, sem_cells).wait()

    def gather(b, g):
        cols = pl.ds(pl.multiple_of(g * 128, 128), 128)
        mine = jnp.logical_and(row[b] == gx, col[b] == gy).astype(F32)
        want = ol[:, cols] * 8 + ox[:, cols]
        want = jnp.broadcast_to(jnp.where(b == 0, want[0:1], want[1:2]), (8, 128))
        at = oy[:, cols]
        at = jnp.broadcast_to(jnp.where(b == 0, at[0:1], at[1:2]), (8, 128))
        for k in range(0, MEMBERS, 8):
            got = jnp.zeros((8, 128), F32)
            for r in range(32):
                moved = jnp.take_along_axis(cells[r, k : k + 8], at, axis=1, mode="promise_in_bounds")
                got = jnp.where(want == r, moved, got)
            piece[b, 2 * g + k // 40, k % 40 : k % 40 + 8] = got * mine

    def remote(src, dst, send, recv, to):
        return pltpu.make_async_remote_copy(
            src_ref=src, dst_ref=dst, send_sem=send, recv_sem=recv, device_id=to, device_id_type=MESH)

    def c0(g):
        two = pl.ds(2 * g, 2)
        return remote(piece.at[other, two], pair_buf.at[two], s0s.at[g], s0r.at[g], mate)

    def c1(t, slot):
        return remote(acc.at[t], ring_buf.at[slot], s1s.at[t], s1r.at[slot], dev_xy(t))

    def c2(t, slot):
        return remote(z_src, z_buf.at[slot], s2s.at[t], s2r.at[slot], dev_z(t))

    def c3(t, slot):
        return remote(full.at[slot], full.at[slot], s3s.at[t], s3r.at[slot], dev_xy(t))

    def c4(b, slot):
        return remote(full.at[slot], out.at[b, slot], s4s.at[slot], s4r.at[slot], mate)

    def keep(slot):
        return pltpu.make_async_copy(full.at[slot], out.at[core, slot], sem_out.at[slot])

    def nth_group(i):
        step = i // 2
        dy = jnp.where(step == 0, 2, jnp.where(step == 1, 1, jnp.where(step == 2, 3, 0)))
        return ((yy + dy) % 4) * 2 + (xx // 2 + 1 + i) % 2

    pl.semaphore_wait(barrier, 23)

    @pl.loop(0, 8)
    def _(i):
        g = nth_group(i)
        gather(other, g)
        c0(g).start()

    @pl.loop(0, 8)
    def _(i):
        g = nth_group(i)
        gather(core, g)
        c0(g).wait_recv()
        for j in range(2):
            t = 2 * g + j
            acc[t] = piece[core, t] + pair_buf[t]

            @pl.when(t != q)
            def _():
                c1(t, q).start()

    total = acc[q]
    for t in behind:
        c1(t, t).wait_recv()
        total = total + ring_buf[t]
    z_src[...] = total
    for d in (4, 3, 5, 2, 6, 1, 7):
        c2((z + d) % 8, z).start()
    for d in (1, 7, 2, 6, 3, 5, 4):
        t = (z + 8 - d) % 8
        c2(t, t).wait_recv()
        total = total + z_buf[t]
    full[q] = total
    for t in ahead:
        c3(t, q).start()
    c4(core, q).start()
    keep(q).start()
    for t in behind:
        c3(t, t).wait_recv()
        c4(core, t).start()
        keep(t).start()

    @pl.loop(0, 16)
    def _(t):
        c4(other, t).wait_recv()

    @pl.loop(0, 8)
    def _(g):
        c0(g).wait_send()

    @pl.loop(0, 16)
    def _(t):
        c4(core, t).wait_send()
        keep(t).wait()

    @pl.loop(1, 16)
    def _(d):
        t = (q + d) % 16
        c1(t, q).wait_send()
        c3(t, q).wait_send()

    @pl.loop(1, 8)
    def _(d):
        c2((z + d) % 8, z).wait_send()


def spread(row, col, state, ox, oy, ol):
    D = pltpu.SemaphoreType.DMA
    S = pltpu.VMEM
    return pl.pallas_call(
        spread_kernel,
        out_shape=jax.ShapeDtypeStruct((2, 16, 40, 128), F32),
        in_specs=[ANY] * 6,
        out_specs=ANY,
        scratch_shapes=[
            pltpu.SMEM((2,), jnp.int32),
            pltpu.SMEM((2,), jnp.int32),
            S((2, 1024), jnp.int32),
            S((2, 1024), jnp.int32),
            S((2, 1024), jnp.int32),
            S((32, MEMBERS, 128), F32),
            S((2, 16, 40, 128), F32),
            S((16, 40, 128), F32),
            S((16, 40, 128), F32),
            S((16, 40, 128), F32),
            S((40, 128), F32),
            S((8, 40, 128), F32),
            S((16, 40, 128), F32),
            D((5,)), D, D((16,)),
            D((8,)), D((8,)), D((16,)), D((16,)), D((8,)), D((8,)), D((16,)), D((16,)), D((16,)), D((16,)),
        ],
        compiler_params=pltpu.CompilerParams(
            collective_id=0, has_side_effects=True, vmem_limit_bytes=60 * 2**20),
    )(row, col, state, ox, oy, ol)


def shards(ensemble, obs_x, obs_y, obs_level, owner_row, owner_col, obs_value, obs_noise, obs_var):
    cells = ensemble.reshape(MEMBERS, 32, 128)
    obs = spread(owner_row, owner_col, cells, obs_x, obs_y, obs_level)
    out = update(owner_row, owner_col, cells, obs, obs_x, obs_y, obs_level, obs_value, obs_noise, obs_var)
    return out.reshape(ensemble.shape)


def solution(mesh):
    in_specs = (P(None, None, "gx", "gy"), P(), P(), P(), P(), P(), P(), P(), P())
    out_specs = P(None, None, "gx", "gy")
    return jax.shard_map(shards, mesh=mesh, in_specs=in_specs, out_specs=out_specs, check_vma=False)
```

```python
import jax
import jax.numpy as jnp
from jax import lax
from jax.experimental import pallas as pl
from jax.experimental.pallas import tpu as pltpu
from jax.sharding import PartitionSpec as P

HIGH = lax.Precision.HIGHEST
F32 = jnp.float32
BF16 = jnp.bfloat16
LOC = 64
MEMBERS = 80
NT = (((1,), (1,)), ((), ()))
NN = (((1,), (0,)), ((), ()))


def split(v):
    hi = v.astype(BF16)
    lo = (v - hi.astype(F32)).astype(BF16)
    return hi, lo


def dot(a, b, dims=NN, precision=None):
    return lax.dot_general(a, b, dims, precision=precision, preferred_element_type=F32)


def inverse_of(a, keep):
    eye = jnp.where(
        lax.broadcasted_iota(jnp.int32, a.shape, 0) == lax.broadcasted_iota(jnp.int32, a.shape, 1), 1.0, 0.0
    )
    top = jnp.max(jnp.sum(jnp.abs(a), axis=1, keepdims=True), axis=0, keepdims=True)
    scale = 2.0 / (top + (MEMBERS - 1.0))
    r = eye - scale * a
    x = scale * (eye + r)
    for _ in range(5):
        r = dot(r, r, NN, HIGH)
        x = x + dot(x, r, NN, HIGH)

    keep[0] = x
    keep[1] = r

    def more(held):
        return jnp.logical_and(held[0] > 1e-4, held[1] < 40)

    def rest(held):
        r = dot(keep[1], keep[1], NN, HIGH)
        keep[0] = keep[0] + dot(keep[0], r, NN, HIGH)
        keep[1] = r
        return jnp.max(jnp.abs(r)), held[1] + 1

    _, count = lax.while_loop(more, rest, (jnp.max(jnp.abs(r)), jnp.int32(0)))

    @pl.when(count > 0)
    def _():
        x = keep[0]
        keep[0] = x + dot(x, eye - dot(a, x, NN, HIGH), NN, HIGH)

    return keep[0]


def update_kernel(row_in, col_in, state, obs_in, ox_in, oy_in, ol_in, value_in, noise_in, var_in, out,
                  row, col, ox, oy, ol, value, var, obs, noises, cells, hx, both, scaled, cast, weights, near_y, col_x, col_y, col_f, taper, keep, gain_hi, gain_lo,
                  sem_in, sem_small, sem_out):
    gx = lax.axis_index("gx")
    gy = lax.axis_index("gy")
    small = [(row_in, row), (col_in, col), (ox_in, ox), (oy_in, oy), (ol_in, ol), (value_in, value), (var_in, var)]
    small += [(obs_in, obs), (noise_in, noises)]
    small = [pltpu.make_async_copy(src, dst, sem_small.at[i]) for i, (src, dst) in enumerate(small)]
    for copy in small:
        copy.start()

    def fetch(r):
        return pltpu.make_async_copy(state.at[:, r], cells.at[r], sem_in)

    def store(r):
        return pltpu.make_async_copy(cells.at[r], out.at[:, r], sem_out)

    @pl.loop(0, 32)
    def _(r):
        fetch(r).start()

    for copy in small[:2]:
        copy.wait()

    def close(b, x, y):
        return jnp.logical_and(jnp.abs(x - row[b]) <= 8, jnp.abs(y - col[b]) <= 1)

    near = [close(b, gx, gy) for b in range(2)]
    linked = jnp.logical_and(near[1], close(0, row[1], col[1]))
    any_near = jnp.logical_or(near[0], near[1])
    all_in = pltpu.make_async_copy(cells, cells, sem_in)
    all_out = pltpu.make_async_copy(cells, cells, sem_out)

    for copy in small[2:]:
        copy.wait()

    @pl.when(linked)
    def _():
        hx[...] = obs[1]

    def members_of(ref, c):
        return jnp.concatenate([ref[2 * c + j] for j in range(2)], axis=0)

    def prepare(b, source):
        lane = lax.broadcasted_iota(jnp.int32, (1, 128), 1)
        mesh_y = (gy * 128 + lane - col[b] * 128).astype(F32) * (1.0 / LOC)

        @pl.loop(0, 8, unroll=4)
        def _(c):
            cols = pl.ds(pl.multiple_of(c * 128, 128), 128)
            h = members_of(source, c)
            inv = 1.0 / var[b : b + 1, cols]
            o = h - jnp.sum(h, axis=0, keepdims=True) * (1.0 / MEMBERS)
            d = value[b : b + 1, cols] + noises[b, :, cols] - h
            both[0:MEMBERS, cols] = o
            both[MEMBERS : 2 * MEMBERS, cols] = d
            for n, part in enumerate((o * inv, d * inv)):
                hi, lo = split(part)
                scaled[n * MEMBERS : (n + 1) * MEMBERS, cols] = hi
                scaled[(n + 2) * MEMBERS : (n + 3) * MEMBERS, cols] = lo
            lev = ol[b : b + 1, cols].astype(F32)
            extra = [ox[b : b + 1, cols].astype(F32) * (1.0 / LOC), oy[b : b + 1, cols].astype(F32) * (1.0 / LOC)]
            for level in range(4):
                extra.append(1.0 / ((1.0 + jnp.abs(level - lev)) * (MEMBERS - 1)))
            extra.append(jnp.zeros((42, 128), F32))
            turned = jnp.concatenate([o] + extra, axis=0).T
            x_at = jnp.broadcast_to(turned[:, 80:81], (128, 128))
            y_at = jnp.broadcast_to(turned[:, 81:82], (128, 128))
            col_x[cols, :] = x_at
            col_y[cols, :] = y_at
            dy = mesh_y - y_at
            near_y[cols, :] = 1.0 - dy * dy
            turned_o = jnp.where(lane < MEMBERS, turned, 0.0)
            first = turned_o + jnp.where(lane >= MEMBERS, pltpu.roll(turned, MEMBERS, 1), 0.0)
            second = jnp.where(lane < 32, pltpu.roll(turned, MEMBERS, 1), 0.0) + pltpu.roll(turned_o, 32, 1)
            for level in range(5):
                if level < 4:
                    f_at = jnp.broadcast_to(turned[:, 82 + level : 83 + level], (128, 128))
                    col_f[level, cols, :] = f_at
                    left, right = first * f_at, second * f_at
                else:
                    left, right = first, second
                hi = right.astype(BF16).astype(F32)
                cast[level, cols, 0:128] = left.astype(BF16)
                cast[level, cols, 128:256] = jnp.where(lane < 32, hi, right - hi).astype(BF16)

        gram = dot(scaled[...], cast[4])
        gram = gram[0:160, 0:80] + gram[0:160, 160:240] + gram[160:320, 0:80]
        inner = gram[0:MEMBERS]
        eye = lax.broadcasted_iota(jnp.int32, (MEMBERS, MEMBERS), 0) == lax.broadcasted_iota(
            jnp.int32, (MEMBERS, MEMBERS), 1
        )
        trace = jnp.sum(jnp.sum(jnp.where(eye, inner, 0.0), axis=1, keepdims=True), axis=0, keepdims=True)
        inner = inner + jnp.where(eye, MEMBERS - 1.0, 0.0) + trace * (1.0 / MEMBERS / MEMBERS)
        inverse = inverse_of(inner, keep)
        factor = dot(gram[MEMBERS : 2 * MEMBERS], inverse, NN, HIGH)
        w = both[MEMBERS : 2 * MEMBERS] - dot(factor, both[0:MEMBERS], NN, HIGH)
        w = w * (1.0 / var[b : b + 1, :])
        hi, lo = split(w)
        weights[0:MEMBERS] = hi
        weights[MEMBERS : 2 * MEMBERS] = lo

    def spread_of(values):
        mean = jnp.sum(values, axis=0, keepdims=True) * (1.0 / MEMBERS)
        hi, lo = split(values - mean)
        return jnp.concatenate([hi, lo, hi, jnp.zeros((16, values.shape[1]), BF16)], axis=0)

    def gain(values, level, taper_at, slot=0):
        right = spread_of(values)
        wide = values.shape[1]
        for part in range(2):
            span = slice(part * 512, part * 512 + 512)
            cross = dot(cast[level, span, :], right)
            hi, lo = split(cross * taper_at(span))
            gain_hi[slot, span, 0:wide] = hi
            gain_lo[slot, span, 0:wide] = lo
        total = dot(weights[...], gain_hi[slot, :, 0:wide])
        rest = dot(weights[0:MEMBERS], gain_lo[slot, :, 0:wide])
        return total[0:MEMBERS] + total[MEMBERS : 2 * MEMBERS] + rest

    def move_state(b, last):
        @pl.loop(0, 4, unroll=2)
        def _(pair):
            x = [(gx * 8 + pair * 2 + half - row[b] * 8).astype(F32) * (1.0 / LOC) for half in range(2)]

            def taper_at(span):
                parts = []
                for half in range(2):
                    dx = x[half] - col_x[span, :]
                    t = jnp.maximum(near_y[span, :] - dx * dx, 0.0)
                    parts.append(t * t)
                t = jnp.concatenate(parts, axis=1)
                taper[span, :] = t
                return t

            before = []
            for level in range(4):
                before.append([cells[level * 8 + pair * 2 + half] for half in range(2)])
            after = []
            for level in range(4):
                change = gain(jnp.concatenate(before[level], axis=1), level, (lambda span: taper[span, :]) if level else taper_at, level % 2)
                after.append([before[level][half] + change[:, half * 128 : half * 128 + 128] for half in range(2)])
            for level in range(4):
                for half in range(2):
                    cells[level * 8 + pair * 2 + half] = after[level][half]
            for level in range(4):
                for half in range(2):
                    r = level * 8 + pair * 2 + half
                    if last is True:
                        store(r).start()
                    else:
                        pl.when(last)(store(r).start)

    def move_obs():
        @pl.loop(0, 4)
        def _(c):
            cols = pl.ds(pl.multiple_of(c * 256, 256), 256)
            x = (ox[1:2, cols] + (row[1] - row[0]) * 8).astype(F32) * (1.0 / LOC)
            y = (oy[1:2, cols] + (col[1] - col[0]) * 128).astype(F32) * (1.0 / LOC)
            lev = ol[1:2, cols]
            at = [lev == level for level in range(3)]

            def taper_at(span):
                parts = []
                for half in range(2):
                    here = slice(half * 128, half * 128 + 128)
                    dx = x[:, here] - col_x[span, :]
                    dy = y[:, here] - col_y[span, :]
                    t = jnp.maximum(1.0 - (dx * dx + dy * dy), 0.0)
                    f = col_f[3, span, :]
                    for level in range(3):
                        f = jnp.where(at[level][:, here], col_f[level, span, :], f)
                    parts.append(t * t * f)
                return jnp.concatenate(parts, axis=1)

            h = jnp.concatenate([members_of(hx, 2 * c + half) for half in range(2)], axis=1)
            h = h + gain(h, 4, taper_at)
            for j in range(4):
                hx[4 * c + j] = h[40 * (j % 2) : 40 * (j % 2) + 40, 128 * (j // 2) : 128 * (j // 2) + 128]

    @pl.when(jnp.logical_or(near[0], linked))
    def _():
        prepare(0, obs.at[0])

    all_in.wait()

    @pl.when(jnp.logical_not(any_near))
    def _():
        @pl.loop(0, 32)
        def _(r):
            store(r).start()

    @pl.when(near[0])
    def _():
        move_state(0, jnp.logical_not(near[1]))

    @pl.when(linked)
    def _():
        move_obs()

    @pl.when(near[1])
    def _():
        @pl.when(jnp.logical_not(linked))
        def _():
            hx[...] = obs[1]

        prepare(1, hx)
        move_state(1, True)

    all_out.wait()


VMEM = pl.BlockSpec(memory_space=pltpu.VMEM)
SMEM = pl.BlockSpec(memory_space=pltpu.SMEM)
ANY = pl.BlockSpec(memory_space=pl.ANY)


def update(row, col, state, obs, ox, oy, ol, value, noise, var):
    S = pltpu.VMEM
    return pl.pallas_call(
        update_kernel,
        out_shape=jax.ShapeDtypeStruct(state.shape, F32),
        in_specs=[ANY] * 10,
        out_specs=ANY,
        scratch_shapes=[
            pltpu.SMEM((2,), jnp.int32),
            pltpu.SMEM((2,), jnp.int32),
            S((2, 1024), jnp.int32),
            S((2, 1024), jnp.int32),
            S((2, 1024), jnp.int32),
            S((2, 1024), F32),
            S((2, 1024), F32),
            S((2, 16, 40, 128), F32),
            S((2, MEMBERS, 1024), F32),
            S((32, MEMBERS, 128), F32),
            S((16, 40, 128), F32),
            S((160, 1024), F32),
            S((4 * MEMBERS, 1024), BF16),
            S((5, 1024, 256), BF16),
            S((160, 1024), BF16),
            S((1024, 128), F32),
            S((1024, 128), F32),
            S((1024, 128), F32),
            S((4, 1024, 128), F32),
            S((1024, 256), F32),
            S((2, MEMBERS, MEMBERS), F32),
            S((2, 1024, 256), BF16),
            S((2, 1024, 256), BF16),
            pltpu.SemaphoreType.DMA,
            pltpu.SemaphoreType.DMA((9,)),
            pltpu.SemaphoreType.DMA,
        ],
        compiler_params=pltpu.CompilerParams(vmem_limit_bytes=60 * 2**20),
    )(row, col, state, obs, ox, oy, ol, value, noise, var)


MESH = pl.DeviceIdType.MESH


FAR = sorted(((dx, dy) for dx in range(4) for dy in range(4) if dx or dy), key=lambda o: -sum(min(d, 4 - d) for d in o))


def spread_kernel(row_in, col_in, state, ox_in, oy_in, ol_in, out,
                  row, col, ox, oy, ol, cells, piece, pair_buf, acc, ring_buf, z_src, z_buf, full,
                  sem, sem_cells, sem_out, s0s, s0r, s1s, s1r, s2s, s2r, s3s, s3r, s4s, s4r):
    gx = lax.axis_index("gx")
    gy = lax.axis_index("gy")
    yy = gx // 4
    zh = gx % 4
    zl = gy // 8
    xx = (gy // 2) % 4
    core = gy % 2
    other = 1 - core
    q = yy * 4 + xx
    z = zh * 2 + zl

    def dev_xy(t):
        return ((t // 4) * 4 + zh, zl * 8 + (t % 4) * 2 + core)

    def dev_z(t):
        return (yy * 4 + t // 2, (t % 2) * 8 + xx * 2 + core)

    mate = (gx, zl * 8 + xx * 2 + other)
    ahead = [((yy + dy) % 4) * 4 + (xx + dx) % 4 for dx, dy in FAR]
    behind = [((yy + 4 - dy) % 4) * 4 + (xx + 4 - dx) % 4 for dx, dy in reversed(FAR)]

    small = [(row_in, row), (col_in, col), (ox_in, ox), (oy_in, oy), (ol_in, ol)]
    small = [pltpu.make_async_copy(src, dst, sem.at[i]) for i, (src, dst) in enumerate(small)]
    for copy in small:
        copy.start()

    @pl.loop(0, 32)
    def _(r):
        pltpu.make_async_copy(state.at[:, r], cells.at[r], sem_cells).start()

    barrier = pltpu.get_barrier_semaphore()

    @pl.loop(1, 16)
    def _(d):
        pl.semaphore_signal(barrier, inc=1, device_id=dev_xy((q + d) % 16), device_id_type=MESH)

    @pl.loop(1, 8)
    def _(d):
        pl.semaphore_signal(barrier, inc=1, device_id=dev_z((z + d) % 8), device_id_type=MESH)

    pl.semaphore_signal(barrier, inc=1, device_id=mate, device_id_type=MESH)

    for copy in small:
        copy.wait()
    pltpu.make_async_copy(cells, cells, sem_cells).wait()

    def gather(b, g):
        cols = pl.ds(pl.multiple_of(g * 128, 128), 128)
        mine = jnp.logical_and(row[b] == gx, col[b] == gy).astype(F32)
        want = ol[:, cols] * 8 + ox[:, cols]
        want = jnp.broadcast_to(jnp.where(b == 0, want[0:1], want[1:2]), (8, 128))
        at = oy[:, cols]
        at = jnp.broadcast_to(jnp.where(b == 0, at[0:1], at[1:2]), (8, 128))
        for k in range(0, MEMBERS, 8):
            got = jnp.zeros((8, 128), F32)
            for r in range(32):
                moved = jnp.take_along_axis(cells[r, k : k + 8], at, axis=1, mode="promise_in_bounds")
                got = jnp.where(want == r, moved, got)
            piece[b, 2 * g + k // 40, k % 40 : k % 40 + 8] = got * mine

    def remote(src, dst, send, recv, to):
        return pltpu.make_async_remote_copy(
            src_ref=src, dst_ref=dst, send_sem=send, recv_sem=recv, device_id=to, device_id_type=MESH)

    def c0(g):
        two = pl.ds(2 * g, 2)
        return remote(piece.at[other, two], pair_buf.at[two], s0s.at[g], s0r.at[g], mate)

    def c1(t, slot):
        return remote(acc.at[t], ring_buf.at[slot], s1s.at[t], s1r.at[slot], dev_xy(t))

    def c2(t, slot):
        return remote(z_src, z_buf.at[slot], s2s.at[t], s2r.at[slot], dev_z(t))

    def c3(t, slot):
        return remote(full.at[slot], full.at[slot], s3s.at[t], s3r.at[slot], dev_xy(t))

    def c4(b, slot):
        return remote(full.at[slot], out.at[b, slot], s4s.at[slot], s4r.at[slot], mate)

    def keep(slot):
        return pltpu.make_async_copy(full.at[slot], out.at[core, slot], sem_out.at[slot])

    def nth_group(i):
        step = i // 2
        dy = jnp.where(step == 0, 2, jnp.where(step == 1, 1, jnp.where(step == 2, 3, 0)))
        return ((yy + dy) % 4) * 2 + (xx // 2 + 1 + i) % 2

    @pl.loop(0, 8)
    def _(i):
        gather(other, nth_group(i))

        @pl.when(i == 5)
        def _():
            pl.semaphore_wait(barrier, 23)

            @pl.loop(0, 5)
            def _(e):
                c0(nth_group(e)).start()

        @pl.when(i >= 5)
        def _():
            c0(nth_group(i)).start()

    @pl.loop(0, 8)
    def _(i):
        g = nth_group(i)
        gather(core, g)
        c0(g).wait_recv()
        for j in range(2):
            t = 2 * g + j
            acc[t] = piece[core, t] + pair_buf[t]

            @pl.when(t != q)
            def _():
                c1(t, q).start()

    total = acc[q]
    for t in behind:
        c1(t, t).wait_recv()
        total = total + ring_buf[t]
    z_src[...] = total
    for d in (4, 3, 5, 2, 6, 1, 7):
        c2((z + d) % 8, z).start()
    for d in (1, 7, 2, 6, 3, 5, 4):
        t = (z + 8 - d) % 8
        c2(t, t).wait_recv()
        total = total + z_buf[t]
    full[q] = total
    for t in ahead:
        c3(t, q).start()
    c4(core, q).start()
    keep(q).start()
    for t in behind:
        c3(t, t).wait_recv()
        c4(core, t).start()
        keep(t).start()

    @pl.loop(0, 16)
    def _(t):
        c4(other, t).wait_recv()

    @pl.loop(0, 8)
    def _(g):
        c0(g).wait_send()

    @pl.loop(0, 16)
    def _(t):
        c4(core, t).wait_send()
        keep(t).wait()

    @pl.loop(1, 16)
    def _(d):
        t = (q + d) % 16
        c1(t, q).wait_send()
        c3(t, q).wait_send()

    @pl.loop(1, 8)
    def _(d):
        c2((z + d) % 8, z).wait_send()


def spread(row, col, state, ox, oy, ol):
    D = pltpu.SemaphoreType.DMA
    S = pltpu.VMEM
    return pl.pallas_call(
        spread_kernel,
        out_shape=jax.ShapeDtypeStruct((2, 16, 40, 128), F32),
        in_specs=[ANY] * 6,
        out_specs=ANY,
        scratch_shapes=[
            pltpu.SMEM((2,), jnp.int32),
            pltpu.SMEM((2,), jnp.int32),
            S((2, 1024), jnp.int32),
            S((2, 1024), jnp.int32),
            S((2, 1024), jnp.int32),
            S((32, MEMBERS, 128), F32),
            S((2, 16, 40, 128), F32),
            S((16, 40, 128), F32),
            S((16, 40, 128), F32),
            S((16, 40, 128), F32),
            S((40, 128), F32),
            S((8, 40, 128), F32),
            S((16, 40, 128), F32),
            D((5,)), D, D((16,)),
            D((8,)), D((8,)), D((16,)), D((16,)), D((8,)), D((8,)), D((16,)), D((16,)), D((16,)), D((16,)),
        ],
        compiler_params=pltpu.CompilerParams(
            collective_id=0, has_side_effects=True, vmem_limit_bytes=60 * 2**20),
    )(row, col, state, ox, oy, ol)


def shards(ensemble, obs_x, obs_y, obs_level, owner_row, owner_col, obs_value, obs_noise, obs_var):
    cells = ensemble.reshape(MEMBERS, 32, 128)
    obs = spread(owner_row, owner_col, cells, obs_x, obs_y, obs_level)
    out = update(owner_row, owner_col, cells, obs, obs_x, obs_y, obs_level, obs_value, obs_noise, obs_var)
    return out.reshape(ensemble.shape)


def solution(mesh):
    in_specs = (P(None, None, "gx", "gy"), P(), P(), P(), P(), P(), P(), P(), P())
    out_specs = P(None, None, "gx", "gy")
    return jax.shard_map(shards, mesh=mesh, in_specs=in_specs, out_specs=out_specs, check_vma=False)
```

```python
import jax
import jax.numpy as jnp
from jax import lax
from jax.experimental import pallas as pl
from jax.experimental.pallas import tpu as pltpu
from jax.sharding import PartitionSpec as P

HIGH = lax.Precision.HIGHEST
F32 = jnp.float32
BF16 = jnp.bfloat16
LOC = 64
MEMBERS = 80
NT = (((1,), (1,)), ((), ()))
NN = (((1,), (0,)), ((), ()))


def split(v):
    hi = v.astype(BF16)
    lo = (v - hi.astype(F32)).astype(BF16)
    return hi, lo


def dot(a, b, dims=NN, precision=None):
    return lax.dot_general(a, b, dims, precision=precision, preferred_element_type=F32)


def inverse_of(a, keep):
    eye = jnp.where(
        lax.broadcasted_iota(jnp.int32, a.shape, 0) == lax.broadcasted_iota(jnp.int32, a.shape, 1), 1.0, 0.0
    )
    top = jnp.max(jnp.sum(jnp.abs(a), axis=1, keepdims=True), axis=0, keepdims=True)
    scale = 2.0 / (top + (MEMBERS - 1.0))
    r = eye - scale * a
    x = scale * (eye + r)
    for _ in range(5):
        r = dot(r, r, NN, HIGH)
        x = x + dot(x, r, NN, HIGH)

    keep[0] = x
    keep[1] = r

    def more(held):
        return jnp.logical_and(held[0] > 1e-4, held[1] < 40)

    def rest(held):
        r = dot(keep[1], keep[1], NN, HIGH)
        keep[0] = keep[0] + dot(keep[0], r, NN, HIGH)
        keep[1] = r
        return jnp.max(jnp.abs(r)), held[1] + 1

    _, count = lax.while_loop(more, rest, (jnp.max(jnp.abs(r)), jnp.int32(0)))

    @pl.when(count > 0)
    def _():
        x = keep[0]
        keep[0] = x + dot(x, eye - dot(a, x, NN, HIGH), NN, HIGH)

    return keep[0]


def update_kernel(row_in, col_in, state, obs_in, ox_in, oy_in, ol_in, value_in, noise_in, var_in, out,
                  row, col, ox, oy, ol, value, var, obs, noises, cells, hx, gap, lines, scaled, cast, weights, near_y, col_x, col_y, col_f, taper, keep, gain_hi, gain_lo,
                  sem_in, sem_small, sem_out):
    gx = lax.axis_index("gx")
    gy = lax.axis_index("gy")
    small = [(row_in, row), (col_in, col), (ox_in, ox), (oy_in, oy), (ol_in, ol), (value_in, value), (var_in, var)]
    small += [(obs_in, obs), (noise_in, noises)]
    small = [pltpu.make_async_copy(src, dst, sem_small.at[i]) for i, (src, dst) in enumerate(small)]
    for copy in small:
        copy.start()

    def fetch(r):
        return pltpu.make_async_copy(state.at[:, r], cells.at[r], sem_in)

    def store(r):
        return pltpu.make_async_copy(cells.at[r], out.at[:, r], sem_out)

    @pl.loop(0, 32)
    def _(r):
        fetch(r).start()

    for copy in small[:2]:
        copy.wait()

    def close(b, x, y):
        return jnp.logical_and(jnp.abs(x - row[b]) <= 8, jnp.abs(y - col[b]) <= 1)

    near = [close(b, gx, gy) for b in range(2)]
    linked = jnp.logical_and(near[1], close(0, row[1], col[1]))
    any_near = jnp.logical_or(near[0], near[1])
    all_in = pltpu.make_async_copy(cells, cells, sem_in)
    all_out = pltpu.make_async_copy(cells, cells, sem_out)

    for copy in small[2:]:
        copy.wait()

    @pl.when(linked)
    def _():
        hx[...] = obs[1]

    def members_of(ref, c):
        return jnp.concatenate([ref[2 * c + j] for j in range(2)], axis=0)

    def prepare(b, source):
        lane = lax.broadcasted_iota(jnp.int32, (1, 128), 1)
        mesh_y = (gy * 128 + lane - col[b] * 128).astype(F32) * (1.0 / LOC)

        @pl.loop(0, 8, unroll=8)
        def _(c):
            cols = pl.ds(pl.multiple_of(c * 128, 128), 128)
            h = members_of(source, c)
            inv = 1.0 / var[b : b + 1, cols]
            o = h - jnp.sum(h, axis=0, keepdims=True) * (1.0 / MEMBERS)
            d = value[b : b + 1, cols] + noises[b, :, cols] - h
            gap[:, cols] = d
            hi, lo = split(o)
            lines[:, cols] = jnp.concatenate([hi, lo, hi, jnp.zeros((16, 128), BF16)], axis=0)
            for n, part in enumerate((o * inv, d * inv)):
                hi, lo = split(part)
                scaled[n * MEMBERS : (n + 1) * MEMBERS, cols] = hi
                scaled[(n + 2) * MEMBERS : (n + 3) * MEMBERS, cols] = lo
            lev = ol[b : b + 1, cols].astype(F32)
            extra = [ox[b : b + 1, cols].astype(F32) * (1.0 / LOC), oy[b : b + 1, cols].astype(F32) * (1.0 / LOC)]
            for level in range(4):
                extra.append(1.0 / ((1.0 + jnp.abs(level - lev)) * (MEMBERS - 1)))
            extra.append(jnp.zeros((42, 128), F32))
            turned = jnp.concatenate([o] + extra, axis=0).T
            x_at = jnp.broadcast_to(turned[:, 80:81], (128, 128))
            y_at = jnp.broadcast_to(turned[:, 81:82], (128, 128))
            col_x[cols, :] = x_at
            col_y[cols, :] = y_at
            dy = mesh_y - y_at
            near_y[cols, :] = 1.0 - dy * dy
            turned_o = jnp.where(lane < MEMBERS, turned, 0.0)
            first = turned_o + jnp.where(lane >= MEMBERS, pltpu.roll(turned, MEMBERS, 1), 0.0)
            second = jnp.where(lane < 32, pltpu.roll(turned, MEMBERS, 1), 0.0) + pltpu.roll(turned_o, 32, 1)
            for level in range(5):
                if level < 4:
                    f_at = jnp.broadcast_to(turned[:, 82 + level : 83 + level], (128, 128))
                    col_f[level, cols, :] = f_at
                    left, right = first * f_at, second * f_at
                else:
                    left, right = first, second
                hi = right.astype(BF16).astype(F32)
                cast[level, cols, 0:128] = left.astype(BF16)
                cast[level, cols, 128:256] = jnp.where(lane < 32, hi, right - hi).astype(BF16)

        gram = dot(scaled[...], cast[4])
        gram = gram[0:160, 0:80] + gram[0:160, 160:240] + gram[160:320, 0:80]
        inner = gram[0:MEMBERS]
        eye = lax.broadcasted_iota(jnp.int32, (MEMBERS, MEMBERS), 0) == lax.broadcasted_iota(
            jnp.int32, (MEMBERS, MEMBERS), 1
        )
        trace = jnp.sum(jnp.sum(jnp.where(eye, inner, 0.0), axis=1, keepdims=True), axis=0, keepdims=True)
        inner = inner + jnp.where(eye, MEMBERS - 1.0, 0.0) + trace * (1.0 / MEMBERS / MEMBERS)
        inverse = inverse_of(inner, keep)
        factor = dot(gram[MEMBERS : 2 * MEMBERS], inverse, NN, HIGH)
        hi = factor.astype(BF16).astype(F32)
        factor = jnp.concatenate([hi, hi, factor - hi, jnp.zeros((MEMBERS, 16), F32)], axis=1).astype(BF16)
        w = gap[...] - dot(factor, lines[...])
        w = w * (1.0 / var[b : b + 1, :])
        hi, lo = split(w)
        weights[0:MEMBERS] = hi
        weights[MEMBERS : 2 * MEMBERS] = lo

    def spread_of(values):
        mean = jnp.sum(values, axis=0, keepdims=True) * (1.0 / MEMBERS)
        hi, lo = split(values - mean)
        return jnp.concatenate([hi, lo, hi, jnp.zeros((16, values.shape[1]), BF16)], axis=0)

    def gain(values, level, taper_at, slot=0):
        right = spread_of(values)
        wide = values.shape[1]
        for part in range(2):
            span = slice(part * 512, part * 512 + 512)
            cross = dot(cast[level, span, :], right)
            hi, lo = split(cross * taper_at(span))
            gain_hi[slot, span, 0:wide] = hi
            gain_lo[slot, span, 0:wide] = lo
        total = dot(weights[...], gain_hi[slot, :, 0:wide])
        rest = dot(weights[0:MEMBERS], gain_lo[slot, :, 0:wide])
        return total[0:MEMBERS] + total[MEMBERS : 2 * MEMBERS] + rest

    def move_state(b, last):
        @pl.loop(0, 4, unroll=2)
        def _(pair):
            x = [(gx * 8 + pair * 2 + half - row[b] * 8).astype(F32) * (1.0 / LOC) for half in range(2)]

            def taper_at(span):
                parts = []
                for half in range(2):
                    dx = x[half] - col_x[span, :]
                    t = jnp.maximum(near_y[span, :] - dx * dx, 0.0)
                    parts.append(t * t)
                t = jnp.concatenate(parts, axis=1)
                taper[span, :] = t
                return t

            before = []
            for level in range(4):
                before.append([cells[level * 8 + pair * 2 + half] for half in range(2)])
            after = []
            for level in range(4):
                change = gain(jnp.concatenate(before[level], axis=1), level, (lambda span: taper[span, :]) if level else taper_at, level % 2)
                after.append([before[level][half] + change[:, half * 128 : half * 128 + 128] for half in range(2)])
            for level in range(4):
                for half in range(2):
                    cells[level * 8 + pair * 2 + half] = after[level][half]
            for level in range(4):
                for half in range(2):
                    r = level * 8 + pair * 2 + half
                    if last is True:
                        store(r).start()
                    else:
                        pl.when(last)(store(r).start)

    def move_obs():
        @pl.loop(0, 4)
        def _(c):
            cols = pl.ds(pl.multiple_of(c * 256, 256), 256)
            x = (ox[1:2, cols] + (row[1] - row[0]) * 8).astype(F32) * (1.0 / LOC)
            y = (oy[1:2, cols] + (col[1] - col[0]) * 128).astype(F32) * (1.0 / LOC)
            lev = ol[1:2, cols]
            at = [lev == level for level in range(3)]

            def taper_at(span):
                parts = []
                for half in range(2):
                    here = slice(half * 128, half * 128 + 128)
                    dx = x[:, here] - col_x[span, :]
                    dy = y[:, here] - col_y[span, :]
                    t = jnp.maximum(1.0 - (dx * dx + dy * dy), 0.0)
                    f = col_f[3, span, :]
                    for level in range(3):
                        f = jnp.where(at[level][:, here], col_f[level, span, :], f)
                    parts.append(t * t * f)
                return jnp.concatenate(parts, axis=1)

            h = jnp.concatenate([members_of(hx, 2 * c + half) for half in range(2)], axis=1)
            h = h + gain(h, 4, taper_at)
            for j in range(4):
                hx[4 * c + j] = h[40 * (j % 2) : 40 * (j % 2) + 40, 128 * (j // 2) : 128 * (j // 2) + 128]

    @pl.when(jnp.logical_or(near[0], linked))
    def _():
        prepare(0, obs.at[0])

    all_in.wait()

    @pl.when(jnp.logical_not(any_near))
    def _():
        @pl.loop(0, 32)
        def _(r):
            store(r).start()

    @pl.when(near[0])
    def _():
        move_state(0, jnp.logical_not(near[1]))

    @pl.when(linked)
    def _():
        move_obs()

    @pl.when(near[1])
    def _():
        @pl.when(jnp.logical_not(linked))
        def _():
            hx[...] = obs[1]

        prepare(1, hx)
        move_state(1, True)

    all_out.wait()


VMEM = pl.BlockSpec(memory_space=pltpu.VMEM)
SMEM = pl.BlockSpec(memory_space=pltpu.SMEM)
ANY = pl.BlockSpec(memory_space=pl.ANY)


def update(row, col, state, obs, ox, oy, ol, value, noise, var):
    S = pltpu.VMEM
    return pl.pallas_call(
        update_kernel,
        out_shape=jax.ShapeDtypeStruct(state.shape, F32),
        in_specs=[ANY] * 10,
        out_specs=ANY,
        scratch_shapes=[
            pltpu.SMEM((2,), jnp.int32),
            pltpu.SMEM((2,), jnp.int32),
            S((2, 1024), jnp.int32),
            S((2, 1024), jnp.int32),
            S((2, 1024), jnp.int32),
            S((2, 1024), F32),
            S((2, 1024), F32),
            S((2, 16, 40, 128), F32),
            S((2, MEMBERS, 1024), F32),
            S((32, MEMBERS, 128), F32),
            S((16, 40, 128), F32),
            S((MEMBERS, 1024), F32),
            S((256, 1024), BF16),
            S((4 * MEMBERS, 1024), BF16),
            S((5, 1024, 256), BF16),
            S((160, 1024), BF16),
            S((1024, 128), F32),
            S((1024, 128), F32),
            S((1024, 128), F32),
            S((4, 1024, 128), F32),
            S((1024, 256), F32),
            S((2, MEMBERS, MEMBERS), F32),
            S((2, 1024, 256), BF16),
            S((2, 1024, 256), BF16),
            pltpu.SemaphoreType.DMA,
            pltpu.SemaphoreType.DMA((9,)),
            pltpu.SemaphoreType.DMA,
        ],
        compiler_params=pltpu.CompilerParams(vmem_limit_bytes=60 * 2**20),
    )(row, col, state, obs, ox, oy, ol, value, noise, var)


MESH = pl.DeviceIdType.MESH


FAR = sorted(((dx, dy) for dx in range(4) for dy in range(4) if dx or dy), key=lambda o: -sum(min(d, 4 - d) for d in o))


def spread_kernel(row_in, col_in, state, ox_in, oy_in, ol_in, out,
                  row, col, ox, oy, ol, cells, piece, pair_buf, acc, ring_buf, z_src, z_buf, full,
                  sem, sem_cells, sem_out, s0s, s0r, s1s, s1r, s2s, s2r, s3s, s3r, s4s, s4r):
    gx = lax.axis_index("gx")
    gy = lax.axis_index("gy")
    yy = gx // 4
    zh = gx % 4
    zl = gy // 8
    xx = (gy // 2) % 4
    core = gy % 2
    other = 1 - core
    q = yy * 4 + xx
    z = zh * 2 + zl

    def dev_xy(t):
        return ((t // 4) * 4 + zh, zl * 8 + (t % 4) * 2 + core)

    def dev_z(t):
        return (yy * 4 + t // 2, (t % 2) * 8 + xx * 2 + core)

    mate = (gx, zl * 8 + xx * 2 + other)
    x_at = [xx] + [(xx + d) % 4 for d in range(1, 4)]
    y_at = [yy] + [(yy + d) % 4 for d in range(1, 4)]
    z_at = [z] + [(z + d) % 8 for d in range(1, 8)]
    ahead = [(x_at[dx], y_at[dy]) for dx, dy in FAR]
    behind = [(x_at[-dx], y_at[-dy]) for dx, dy in reversed(FAR)]

    def dev(x, y):
        return (y * 4 + zh, zl * 8 + x * 2 + core)

    barrier = pltpu.get_barrier_semaphore()

    def greet(to):
        pl.semaphore_signal(barrier, inc=1, device_id=to, device_id_type=MESH)

    for d in (4, 3, 5, 2, 6, 1, 7):
        greet(dev_z(z_at[d]))
    for x, y in ahead:
        greet(dev(x, y))
    greet(mate)

    small = [(row_in, row), (col_in, col), (ox_in, ox), (oy_in, oy), (ol_in, ol)]
    small = [pltpu.make_async_copy(src, dst, sem.at[i]) for i, (src, dst) in enumerate(small)]
    for copy in small:
        copy.start()

    @pl.loop(0, 32)
    def _(r):
        pltpu.make_async_copy(state.at[:, r], cells.at[r], sem_cells).start()

    for copy in small:
        copy.wait()
    pltpu.make_async_copy(cells, cells, sem_cells).wait()

    def gather(b, g):
        cols = pl.ds(pl.multiple_of(g * 128, 128), 128)
        mine = jnp.logical_and(row[b] == gx, col[b] == gy).astype(F32)
        want = ol[:, cols] * 8 + ox[:, cols]
        want = jnp.broadcast_to(jnp.where(b == 0, want[0:1], want[1:2]), (8, 128))
        at = oy[:, cols]
        at = jnp.broadcast_to(jnp.where(b == 0, at[0:1], at[1:2]), (8, 128))
        for k in range(0, MEMBERS, 8):
            got = jnp.zeros((8, 128), F32)
            for r in range(32):
                moved = jnp.take_along_axis(cells[r, k : k + 8], at, axis=1, mode="promise_in_bounds")
                got = jnp.where(want == r, moved, got)
            piece[b, 2 * g + k // 40, k % 40 : k % 40 + 8] = got * mine

    def remote(src, dst, send, recv, to):
        return pltpu.make_async_remote_copy(
            src_ref=src, dst_ref=dst, send_sem=send, recv_sem=recv, device_id=to, device_id_type=MESH)

    def c0(g):
        two = pl.ds(2 * g, 2)
        return remote(piece.at[other, two], pair_buf.at[two], s0s.at[g], s0r.at[g], mate)

    def c1(t, slot):
        return remote(acc.at[t], ring_buf.at[slot], s1s.at[t], s1r.at[slot], dev_xy(t))

    def c2(t, slot):
        return remote(z_src, z_buf.at[slot], s2s.at[t], s2r.at[slot], dev_z(t))

    def c3(x, y, slot):
        return remote(full.at[slot], full.at[slot], s3s.at[y * 4 + x], s3r.at[slot], dev(x, y))

    def c4(b, slot):
        return remote(full.at[slot], out.at[b, slot], s4s.at[slot], s4r.at[slot], mate)

    def keep(slot):
        return pltpu.make_async_copy(full.at[slot], out.at[core, slot], sem_out.at[slot])

    def nth_group(i):
        step = i // 2
        dy = jnp.where(step == 0, 2, jnp.where(step == 1, 1, jnp.where(step == 2, 3, 0)))
        return ((yy + dy) % 4) * 2 + (xx // 2 + 1 + i) % 2

    @pl.loop(0, 8)
    def _(i):
        gather(other, nth_group(i))

        @pl.when(i == 5)
        def _():
            pl.semaphore_wait(barrier, 23)

            @pl.loop(0, 5)
            def _(e):
                c0(nth_group(e)).start()

        @pl.when(i >= 5)
        def _():
            c0(nth_group(i)).start()

    @pl.loop(0, 8)
    def _(i):
        g = nth_group(i)
        gather(core, g)
        c0(g).wait_recv()
        for j in range(2):
            t = 2 * g + j
            acc[t] = piece[core, t] + pair_buf[t]

            @pl.when(t != q)
            def _():
                c1(t, q).start()

    total = acc[q]
    for x, y in behind:
        t = y * 4 + x
        c1(t, t).wait_recv()
        total = total + ring_buf[t]
    z_src[...] = total
    for d in (4, 3, 5, 2, 6, 1, 7):
        c2(z_at[d], z).start()
    for d in (1, 7, 2, 6, 3, 5, 4):
        t = z_at[-d]
        c2(t, t).wait_recv()
        total = total + z_buf[t]
    full[q] = total
    for x, y in ahead:
        c3(x, y, q).start()
    c4(core, q).start()
    keep(q).start()
    for x, y in behind:
        t = y * 4 + x
        c3(x, y, t).wait_recv()
        c4(core, t).start()
        keep(t).start()

    @pl.loop(0, 16)
    def _(t):
        c4(other, t).wait_recv()

    @pl.loop(0, 8)
    def _(g):
        c0(g).wait_send()

    @pl.loop(0, 16)
    def _(t):
        c4(core, t).wait_send()
        keep(t).wait()

    @pl.loop(1, 16)
    def _(d):
        t = (q + d) % 16
        c1(t, q).wait_send()
        c3(t % 4, t // 4, q).wait_send()

    @pl.loop(1, 8)
    def _(d):
        c2((z + d) % 8, z).wait_send()


def spread(row, col, state, ox, oy, ol):
    D = pltpu.SemaphoreType.DMA
    S = pltpu.VMEM
    return pl.pallas_call(
        spread_kernel,
        out_shape=jax.ShapeDtypeStruct((2, 16, 40, 128), F32),
        in_specs=[ANY] * 6,
        out_specs=ANY,
        scratch_shapes=[
            pltpu.SMEM((2,), jnp.int32),
            pltpu.SMEM((2,), jnp.int32),
            S((2, 1024), jnp.int32),
            S((2, 1024), jnp.int32),
            S((2, 1024), jnp.int32),
            S((32, MEMBERS, 128), F32),
            S((2, 16, 40, 128), F32),
            S((16, 40, 128), F32),
            S((16, 40, 128), F32),
            S((16, 40, 128), F32),
            S((40, 128), F32),
            S((8, 40, 128), F32),
            S((16, 40, 128), F32),
            D((5,)), D, D((16,)),
            D((8,)), D((8,)), D((16,)), D((16,)), D((8,)), D((8,)), D((16,)), D((16,)), D((16,)), D((16,)),
        ],
        compiler_params=pltpu.CompilerParams(
            collective_id=0, has_side_effects=True, vmem_limit_bytes=60 * 2**20),
    )(row, col, state, ox, oy, ol)


def shards(ensemble, obs_x, obs_y, obs_level, owner_row, owner_col, obs_value, obs_noise, obs_var):
    cells = ensemble.reshape(MEMBERS, 32, 128)
    obs = spread(owner_row, owner_col, cells, obs_x, obs_y, obs_level)
    out = update(owner_row, owner_col, cells, obs, obs_x, obs_y, obs_level, obs_value, obs_noise, obs_var)
    return out.reshape(ensemble.shape)


def solution(mesh):
    in_specs = (P(None, None, "gx", "gy"), P(), P(), P(), P(), P(), P(), P(), P())
    out_specs = P(None, None, "gx", "gy")
    return jax.shard_map(shards, mesh=mesh, in_specs=in_specs, out_specs=out_specs, check_vma=False)
```

```python
import jax
import jax.numpy as jnp
from jax import lax
from jax.experimental import pallas as pl
from jax.experimental.pallas import tpu as pltpu
from jax.sharding import PartitionSpec as P

HIGH = lax.Precision.HIGHEST
F32 = jnp.float32
BF16 = jnp.bfloat16
LOC = 64
MEMBERS = 80
NT = (((1,), (1,)), ((), ()))
NN = (((1,), (0,)), ((), ()))


def split(v):
    hi = v.astype(BF16)
    lo = (v - hi.astype(F32)).astype(BF16)
    return hi, lo


def dot(a, b, dims=NN, precision=None):
    return lax.dot_general(a, b, dims, precision=precision, preferred_element_type=F32)


def inverse_of(a, keep):
    eye = jnp.where(
        lax.broadcasted_iota(jnp.int32, a.shape, 0) == lax.broadcasted_iota(jnp.int32, a.shape, 1), 1.0, 0.0
    )
    top = jnp.max(jnp.sum(jnp.abs(a), axis=1, keepdims=True), axis=0, keepdims=True)
    scale = 2.0 / (top + (MEMBERS - 1.0))
    r = eye - scale * a
    x = scale * (eye + r)
    for _ in range(5):
        r = dot(r, r, NN, HIGH)
        x = x + dot(x, r, NN, HIGH)

    keep[0] = x
    keep[1] = r

    def more(held):
        return jnp.logical_and(held[0] > 1e-4, held[1] < 40)

    def rest(held):
        r = dot(keep[1], keep[1], NN, HIGH)
        keep[0] = keep[0] + dot(keep[0], r, NN, HIGH)
        keep[1] = r
        return jnp.max(jnp.abs(r)), held[1] + 1

    _, count = lax.while_loop(more, rest, (jnp.max(jnp.abs(r)), jnp.int32(0)))

    @pl.when(count > 0)
    def _():
        x = keep[0]
        keep[0] = x + dot(x, eye - dot(a, x, NN, HIGH), NN, HIGH)

    return keep[0]


def update_kernel(row_in, col_in, state, obs_in, ox_in, oy_in, ol_in, value_in, noise_in, var_in, out,
                  row, col, ox, oy, ol, value, var, obs, noises, cells, hx, gap, lines, scaled, cast, weights, near_y, col_x, col_y, col_f, taper, keep, gain_hi, gain_lo,
                  sem_in, sem_small, sem_out):
    gx = lax.axis_index("gx")
    gy = lax.axis_index("gy")
    small = [(row_in, row), (col_in, col), (ox_in, ox), (oy_in, oy), (ol_in, ol), (value_in, value), (var_in, var)]
    small += [(obs_in, obs), (noise_in, noises)]
    small = [pltpu.make_async_copy(src, dst, sem_small.at[i]) for i, (src, dst) in enumerate(small)]
    for copy in small:
        copy.start()

    def fetch(r):
        return pltpu.make_async_copy(state.at[:, r], cells.at[r], sem_in)

    def store(r):
        return pltpu.make_async_copy(cells.at[r], out.at[:, r], sem_out)

    @pl.loop(0, 32)
    def _(r):
        fetch(r).start()

    for copy in small[:2]:
        copy.wait()

    def close(b, x, y):
        return jnp.logical_and(jnp.abs(x - row[b]) <= 8, jnp.abs(y - col[b]) <= 1)

    near = [close(b, gx, gy) for b in range(2)]
    linked = jnp.logical_and(near[1], close(0, row[1], col[1]))
    any_near = jnp.logical_or(near[0], near[1])
    all_in = pltpu.make_async_copy(cells, cells, sem_in)
    all_out = pltpu.make_async_copy(cells, cells, sem_out)

    for copy in small[2:]:
        copy.wait()

    @pl.when(linked)
    def _():
        hx[...] = obs[1]

    def members_of(ref, c):
        return jnp.concatenate([ref[2 * c + j] for j in range(2)], axis=0)

    def prepare(b, source):
        lane = lax.broadcasted_iota(jnp.int32, (1, 128), 1)
        mesh_y = (gy * 128 + lane - col[b] * 128).astype(F32) * (1.0 / LOC)

        @pl.loop(0, 8, unroll=8)
        def _(c):
            cols = pl.ds(pl.multiple_of(c * 128, 128), 128)
            h = members_of(source, c)
            inv = 1.0 / var[b : b + 1, cols]
            o = h - jnp.sum(h, axis=0, keepdims=True) * (1.0 / MEMBERS)
            d = value[b : b + 1, cols] + noises[b, :, cols] - h
            gap[:, cols] = d
            hi, lo = split(o)
            lines[:, cols] = jnp.concatenate([hi, lo, hi, jnp.zeros((16, 128), BF16)], axis=0)
            for n, part in enumerate((o * inv, d * inv)):
                hi, lo = split(part)
                scaled[n * MEMBERS : (n + 1) * MEMBERS, cols] = hi
                scaled[(n + 2) * MEMBERS : (n + 3) * MEMBERS, cols] = lo
            lev = ol[b : b + 1, cols].astype(F32)
            extra = [ox[b : b + 1, cols].astype(F32) * (1.0 / LOC), oy[b : b + 1, cols].astype(F32) * (1.0 / LOC)]
            for level in range(4):
                extra.append(1.0 / ((1.0 + jnp.abs(level - lev)) * (MEMBERS - 1)))
            extra.append(jnp.zeros((42, 128), F32))
            turned = jnp.concatenate([o] + extra, axis=0).T
            x_at = jnp.broadcast_to(turned[:, 80:81], (128, 128))
            y_at = jnp.broadcast_to(turned[:, 81:82], (128, 128))
            col_x[cols, :] = x_at
            col_y[cols, :] = y_at
            dy = mesh_y - y_at
            near_y[cols, :] = 1.0 - dy * dy
            turned_o = jnp.where(lane < MEMBERS, turned, 0.0)
            first = turned_o + jnp.where(lane >= MEMBERS, pltpu.roll(turned, MEMBERS, 1), 0.0)
            second = jnp.where(lane < 32, pltpu.roll(turned, MEMBERS, 1), 0.0) + pltpu.roll(turned_o, 32, 1)
            for level in range(5):
                if level < 4:
                    f_at = jnp.broadcast_to(turned[:, 82 + level : 83 + level], (128, 128))
                    col_f[level, cols, :] = f_at
                    left, right = first * f_at, second * f_at
                else:
                    left, right = first, second
                hi = right.astype(BF16).astype(F32)
                cast[level, cols, 0:128] = left.astype(BF16)
                cast[level, cols, 128:256] = jnp.where(lane < 32, hi, right - hi).astype(BF16)

        gram = dot(scaled[...], cast[4])
        gram = gram[0:160, 0:80] + gram[0:160, 160:240] + gram[160:320, 0:80]
        inner = gram[0:MEMBERS]
        eye = lax.broadcasted_iota(jnp.int32, (MEMBERS, MEMBERS), 0) == lax.broadcasted_iota(
            jnp.int32, (MEMBERS, MEMBERS), 1
        )
        trace = jnp.sum(jnp.sum(jnp.where(eye, inner, 0.0), axis=1, keepdims=True), axis=0, keepdims=True)
        inner = inner + jnp.where(eye, MEMBERS - 1.0, 0.0) + trace * (1.0 / MEMBERS / MEMBERS)
        inverse = inverse_of(inner, keep)
        factor = dot(gram[MEMBERS : 2 * MEMBERS], inverse, NN, HIGH)
        hi = factor.astype(BF16).astype(F32)
        factor = jnp.concatenate([hi, hi, factor - hi, jnp.zeros((MEMBERS, 16), F32)], axis=1).astype(BF16)
        w = gap[...] - dot(factor, lines[...])
        w = w * (1.0 / var[b : b + 1, :])
        hi, lo = split(w)
        weights[0:MEMBERS] = hi
        weights[MEMBERS : 2 * MEMBERS] = lo

    def spread_of(values):
        mean = jnp.sum(values, axis=0, keepdims=True) * (1.0 / MEMBERS)
        hi, lo = split(values - mean)
        return jnp.concatenate([hi, lo, hi, jnp.zeros((16, values.shape[1]), BF16)], axis=0)

    def gain(values, level, taper_at, slot=0):
        right = spread_of(values)
        wide = values.shape[1]
        for part in range(2):
            span = slice(part * 512, part * 512 + 512)
            cross = dot(cast[level, span, :], right)
            hi, lo = split(cross * taper_at(span))
            gain_hi[slot, span, 0:wide] = hi
            gain_lo[slot, span, 0:wide] = lo
        total = dot(weights[...], gain_hi[slot, :, 0:wide])
        rest = dot(weights[0:MEMBERS], gain_lo[slot, :, 0:wide])
        return total[0:MEMBERS] + total[MEMBERS : 2 * MEMBERS] + rest

    def move_state(b, last):
        @pl.loop(0, 4, unroll=4)
        def _(pair):
            x = [(gx * 8 + pair * 2 + half - row[b] * 8).astype(F32) * (1.0 / LOC) for half in range(2)]

            def taper_at(span):
                parts = []
                for half in range(2):
                    dx = x[half] - col_x[span, :]
                    t = jnp.maximum(near_y[span, :] - dx * dx, 0.0)
                    parts.append(t * t)
                t = jnp.concatenate(parts, axis=1)
                taper[span, :] = t
                return t

            before = []
            for level in range(4):
                before.append([cells[level * 8 + pair * 2 + half] for half in range(2)])
            after = []
            for level in range(4):
                change = gain(jnp.concatenate(before[level], axis=1), level, (lambda span: taper[span, :]) if level else taper_at, level % 2)
                after.append([before[level][half] + change[:, half * 128 : half * 128 + 128] for half in range(2)])
            for level in range(4):
                for half in range(2):
                    cells[level * 8 + pair * 2 + half] = after[level][half]
            for level in range(4):
                for half in range(2):
                    r = level * 8 + pair * 2 + half
                    if last is True:
                        store(r).start()
                    else:
                        pl.when(last)(store(r).start)

    def move_obs():
        @pl.loop(0, 4, unroll=2)
        def _(c):
            cols = pl.ds(pl.multiple_of(c * 256, 256), 256)
            x = (ox[1:2, cols] + (row[1] - row[0]) * 8).astype(F32) * (1.0 / LOC)
            y = (oy[1:2, cols] + (col[1] - col[0]) * 128).astype(F32) * (1.0 / LOC)
            lev = ol[1:2, cols]
            at = [lev == level for level in range(3)]

            def taper_at(span):
                parts = []
                for half in range(2):
                    here = slice(half * 128, half * 128 + 128)
                    dx = x[:, here] - col_x[span, :]
                    dy = y[:, here] - col_y[span, :]
                    t = jnp.maximum(1.0 - (dx * dx + dy * dy), 0.0)
                    f = col_f[3, span, :]
                    for level in range(3):
                        f = jnp.where(at[level][:, here], col_f[level, span, :], f)
                    parts.append(t * t * f)
                return jnp.concatenate(parts, axis=1)

            h = jnp.concatenate([members_of(hx, 2 * c + half) for half in range(2)], axis=1)
            h = h + gain(h, 4, taper_at)
            for j in range(4):
                hx[4 * c + j] = h[40 * (j % 2) : 40 * (j % 2) + 40, 128 * (j // 2) : 128 * (j // 2) + 128]

    @pl.when(jnp.logical_or(near[0], linked))
    def _():
        prepare(0, obs.at[0])

    all_in.wait()

    @pl.when(jnp.logical_not(any_near))
    def _():
        @pl.loop(0, 32)
        def _(r):
            store(r).start()

    @pl.when(near[0])
    def _():
        move_state(0, jnp.logical_not(near[1]))

    @pl.when(linked)
    def _():
        move_obs()

    @pl.when(near[1])
    def _():
        @pl.when(jnp.logical_not(linked))
        def _():
            hx[...] = obs[1]

        prepare(1, hx)
        move_state(1, True)

    all_out.wait()


VMEM = pl.BlockSpec(memory_space=pltpu.VMEM)
SMEM = pl.BlockSpec(memory_space=pltpu.SMEM)
ANY = pl.BlockSpec(memory_space=pl.ANY)


def update(row, col, state, obs, ox, oy, ol, value, noise, var):
    S = pltpu.VMEM
    return pl.pallas_call(
        update_kernel,
        out_shape=jax.ShapeDtypeStruct(state.shape, F32),
        in_specs=[ANY] * 10,
        out_specs=ANY,
        scratch_shapes=[
            pltpu.SMEM((2,), jnp.int32),
            pltpu.SMEM((2,), jnp.int32),
            S((2, 1024), jnp.int32),
            S((2, 1024), jnp.int32),
            S((2, 1024), jnp.int32),
            S((2, 1024), F32),
            S((2, 1024), F32),
            S((2, 16, 40, 128), F32),
            S((2, MEMBERS, 1024), F32),
            S((32, MEMBERS, 128), F32),
            S((16, 40, 128), F32),
            S((MEMBERS, 1024), F32),
            S((256, 1024), BF16),
            S((4 * MEMBERS, 1024), BF16),
            S((5, 1024, 256), BF16),
            S((160, 1024), BF16),
            S((1024, 128), F32),
            S((1024, 128), F32),
            S((1024, 128), F32),
            S((4, 1024, 128), F32),
            S((1024, 256), F32),
            S((2, MEMBERS, MEMBERS), F32),
            S((2, 1024, 256), BF16),
            S((2, 1024, 256), BF16),
            pltpu.SemaphoreType.DMA,
            pltpu.SemaphoreType.DMA((9,)),
            pltpu.SemaphoreType.DMA,
        ],
        compiler_params=pltpu.CompilerParams(vmem_limit_bytes=60 * 2**20),
    )(row, col, state, obs, ox, oy, ol, value, noise, var)


MESH = pl.DeviceIdType.MESH


FAR = sorted(((dx, dy) for dx in range(4) for dy in range(4) if dx or dy), key=lambda o: -sum(min(d, 4 - d) for d in o))


def spread_kernel(row_in, col_in, state, ox_in, oy_in, ol_in, out,
                  row, col, ox, oy, ol, cells, piece, pair_buf, acc, ring_buf, z_src, z_buf, full,
                  sem, sem_cells, sem_out, s0s, s0r, s1s, s1r, s2s, s2r, s3s, s3r, s4s, s4r):
    gx = lax.axis_index("gx")
    gy = lax.axis_index("gy")
    yy = gx // 4
    zh = gx % 4
    zl = gy // 8
    xx = (gy // 2) % 4
    core = gy % 2
    other = 1 - core
    q = yy * 4 + xx
    z = zh * 2 + zl

    def dev_xy(t):
        return ((t // 4) * 4 + zh, zl * 8 + (t % 4) * 2 + core)

    def dev_z(t):
        return (yy * 4 + t // 2, (t % 2) * 8 + xx * 2 + core)

    mate = (gx, zl * 8 + xx * 2 + other)
    x_at = [xx] + [(xx + d) % 4 for d in range(1, 4)]
    y_at = [yy] + [(yy + d) % 4 for d in range(1, 4)]
    z_at = [z] + [(z + d) % 8 for d in range(1, 8)]
    ahead = [(x_at[dx], y_at[dy]) for dx, dy in FAR]
    behind = [(x_at[-dx], y_at[-dy]) for dx, dy in reversed(FAR)]

    def dev(x, y):
        return (y * 4 + zh, zl * 8 + x * 2 + core)

    barrier = pltpu.get_barrier_semaphore()

    def greet(to):
        pl.semaphore_signal(barrier, inc=1, device_id=to, device_id_type=MESH)

    for d in (4, 3, 5, 2, 6, 1, 7):
        greet(dev_z(z_at[d]))
    for x, y in ahead:
        greet(dev(x, y))
    greet(mate)

    small = [(row_in, row), (col_in, col), (ox_in, ox), (oy_in, oy), (ol_in, ol)]
    small = [pltpu.make_async_copy(src, dst, sem.at[i]) for i, (src, dst) in enumerate(small)]
    for copy in small:
        copy.start()

    @pl.loop(0, 32)
    def _(r):
        pltpu.make_async_copy(state.at[:, r], cells.at[r], sem_cells).start()

    for copy in small:
        copy.wait()
    pltpu.make_async_copy(cells, cells, sem_cells).wait()

    def gather(b, g):
        cols = pl.ds(pl.multiple_of(g * 128, 128), 128)
        mine = jnp.logical_and(row[b] == gx, col[b] == gy).astype(F32)
        want = ol[:, cols] * 8 + ox[:, cols]
        want = jnp.broadcast_to(jnp.where(b == 0, want[0:1], want[1:2]), (8, 128))
        at = oy[:, cols]
        at = jnp.broadcast_to(jnp.where(b == 0, at[0:1], at[1:2]), (8, 128))
        for k in range(0, MEMBERS, 8):
            got = jnp.zeros((8, 128), F32)
            for r in range(32):
                moved = jnp.take_along_axis(cells[r, k : k + 8], at, axis=1, mode="promise_in_bounds")
                got = jnp.where(want == r, moved, got)
            piece[b, 2 * g + k // 40, k % 40 : k % 40 + 8] = got * mine

    def remote(src, dst, send, recv, to):
        return pltpu.make_async_remote_copy(
            src_ref=src, dst_ref=dst, send_sem=send, recv_sem=recv, device_id=to, device_id_type=MESH)

    def c0(g):
        two = pl.ds(2 * g, 2)
        return remote(piece.at[other, two], pair_buf.at[two], s0s.at[g], s0r.at[g], mate)

    def c1(t, slot):
        return remote(acc.at[t], ring_buf.at[slot], s1s.at[t], s1r.at[slot], dev_xy(t))

    def c2(t, slot):
        return remote(z_src, z_buf.at[slot], s2s.at[t], s2r.at[slot], dev_z(t))

    def c3(x, y, slot):
        return remote(full.at[slot], full.at[slot], s3s.at[y * 4 + x], s3r.at[slot], dev(x, y))

    def c4(b, slot):
        return remote(full.at[slot], out.at[b, slot], s4s.at[slot], s4r.at[slot], mate)

    def keep(slot):
        return pltpu.make_async_copy(full.at[slot], out.at[core, slot], sem_out.at[slot])

    def nth_group(i):
        step = i // 2
        dy = jnp.where(step == 0, 2, jnp.where(step == 1, 1, jnp.where(step == 2, 3, 0)))
        return ((yy + dy) % 4) * 2 + (xx // 2 + 1 + i) % 2

    @pl.loop(0, 8)
    def _(i):
        gather(other, nth_group(i))

        @pl.when(i == 5)
        def _():
            pl.semaphore_wait(barrier, 23)

            @pl.loop(0, 5)
            def _(e):
                c0(nth_group(e)).start()

        @pl.when(i >= 5)
        def _():
            c0(nth_group(i)).start()

    @pl.loop(0, 8)
    def _(i):
        g = nth_group(i)
        gather(core, g)
        c0(g).wait_recv()
        for j in range(2):
            t = 2 * g + j
            acc[t] = piece[core, t] + pair_buf[t]

            @pl.when(t != q)
            def _():
                c1(t, q).start()

    total = acc[q]
    for x, y in behind:
        t = y * 4 + x
        c1(t, t).wait_recv()
        total = total + ring_buf[t]
    z_src[...] = total
    for d in (4, 3, 5, 2, 6, 1, 7):
        c2(z_at[d], z).start()
    for d in (1, 7, 2, 6, 3, 5, 4):
        t = z_at[-d]
        c2(t, t).wait_recv()
        total = total + z_buf[t]
    full[q] = total
    for x, y in ahead:
        c3(x, y, q).start()
    c4(core, q).start()
    keep(q).start()
    for x, y in behind:
        t = y * 4 + x
        c3(x, y, t).wait_recv()
        c4(core, t).start()
        keep(t).start()

    @pl.loop(0, 16)
    def _(t):
        c4(other, t).wait_recv()

    @pl.loop(0, 8)
    def _(g):
        c0(g).wait_send()

    @pl.loop(0, 16)
    def _(t):
        c4(core, t).wait_send()
        keep(t).wait()

    @pl.loop(1, 16)
    def _(d):
        t = (q + d) % 16
        c1(t, q).wait_send()
        c3(t % 4, t // 4, q).wait_send()

    @pl.loop(1, 8)
    def _(d):
        c2((z + d) % 8, z).wait_send()


def spread(row, col, state, ox, oy, ol):
    D = pltpu.SemaphoreType.DMA
    S = pltpu.VMEM
    return pl.pallas_call(
        spread_kernel,
        out_shape=jax.ShapeDtypeStruct((2, 16, 40, 128), F32),
        in_specs=[ANY] * 6,
        out_specs=ANY,
        scratch_shapes=[
            pltpu.SMEM((2,), jnp.int32),
            pltpu.SMEM((2,), jnp.int32),
            S((2, 1024), jnp.int32),
            S((2, 1024), jnp.int32),
            S((2, 1024), jnp.int32),
            S((32, MEMBERS, 128), F32),
            S((2, 16, 40, 128), F32),
            S((16, 40, 128), F32),
            S((16, 40, 128), F32),
            S((16, 40, 128), F32),
            S((40, 128), F32),
            S((8, 40, 128), F32),
            S((16, 40, 128), F32),
            D((5,)), D, D((16,)),
            D((8,)), D((8,)), D((16,)), D((16,)), D((8,)), D((8,)), D((16,)), D((16,)), D((16,)), D((16,)),
        ],
        compiler_params=pltpu.CompilerParams(
            collective_id=0, has_side_effects=True, vmem_limit_bytes=60 * 2**20),
    )(row, col, state, ox, oy, ol)


def shards(ensemble, obs_x, obs_y, obs_level, owner_row, owner_col, obs_value, obs_noise, obs_var):
    cells = ensemble.reshape(MEMBERS, 32, 128)
    obs = spread(owner_row, owner_col, cells, obs_x, obs_y, obs_level)
    out = update(owner_row, owner_col, cells, obs, obs_x, obs_y, obs_level, obs_value, obs_noise, obs_var)
    return out.reshape(ensemble.shape)


def solution(mesh):
    in_specs = (P(None, None, "gx", "gy"), P(), P(), P(), P(), P(), P(), P(), P())
    out_specs = P(None, None, "gx", "gy")
    return jax.shard_map(shards, mesh=mesh, in_specs=in_specs, out_specs=out_specs, check_vma=False)
```
